32 devices in a mesh: groups: 2 (over x), expert: 8 (over z, y), dp: 2 (over core).
Axes of the slice: x: 2, y: 2, z: 4, core: 2. Of those that a mesh axis runs over, the one named last changes fastest.
Arguments:
- tokens: bfloat16 [4096, 3584], P(('groups', 'expert', 'dp')), parts along dimension 0, may hold values from -6 to 6
- grad_out: bfloat16 [4096, 3584], P(('groups', 'expert', 'dp')), parts along dimension 0, may hold values from -6 to 6
- expert_ids: int32 [4096, 8], P(('groups', 'expert', 'dp')), parts along dimension 0, may hold values from 0 to 255, as said below
- gate_weights: float32 [4096, 8], P(('groups', 'expert', 'dp')), parts along dimension 0, may hold values from 0.05 to 0.6
- w_gate: bfloat16 [2048, 3584], P(('expert', 'dp')), may hold values from -0.09375 to 0.09375
- w_up: bfloat16 [2048, 3584], P(('expert', 'dp')), may hold values from -0.09375 to 0.09375
- w_down: bfloat16 [2048, 3584], P(('expert', 'dp')), may hold values from -0.1875 to 0.1875
Outputs:
- grad_tokens: bfloat16 [4096, 3584], P(('groups', 'expert', 'dp')), parts along dimension 0
- grad_gates: float32 [4096, 8], P(('groups', 'expert', 'dp')), parts along dimension 0
- grad_w_gate: bfloat16 [4096, 3584], P(('groups', 'expert', 'dp')), parts along dimension 0
- grad_w_up: bfloat16 [4096, 3584], P(('groups', 'expert', 'dp')), parts along dimension 0
- grad_w_down: bfloat16 [4096, 3584], P(('groups', 'expert', 'dp')), parts along dimension 0
The draws below stay inside these ranges and needn't reach their ends.
There are 2 independent parts, one for each index of `groups`. The reference program is written for one: setup_inputs(seed, part) draws one part's arguments, and reference() takes and returns one part's arrays. A program takes and returns all parts, laid end to end along the dimension named above; an argument that names none is the same for every part. Nothing has to cross between parts.
Inputs may be any that keep to these rules, and one draw needn't show every extreme that they name: `expert_ids`: each row names 8 different experts. Each token names at most one expert below 2. Among the 128 rows of one device no expert below 2 is named by more than 6 rows, and on every device some such expert is named by exactly 6 rows.
All inputs are finite; a program needn't handle non-finite values.
Results may differ from the reference program's by a relative error of at most 0.017.
Values may be sent and summed in bfloat16 or wider, within the bound.
A program may use at most 128 MiB of HBM per device.

```python
import jax
import jax.numpy as jnp
from jax import lax

D = 3584
I_WIN = 1024
EXPERTS_ALL = 256
TOP = 8
TOK_DEV = 128
EXP_WIN = 2
CAP = 6
TOKENS = 2048


def draw_expert_ids(key, part):
    key = jax.random.fold_in(key, 7)
    block_count = TOKENS // TOK_DEV
    subkeys = jax.random.split(key, 5)
    counts = jax.random.randint(subkeys[0], (block_count, EXP_WIN), 0, CAP + 1)
    hottest = jax.random.randint(subkeys[1], (block_count,), 0, EXP_WIN)
    counts = jnp.where(jnp.arange(EXP_WIN)[None, :] == hottest[:, None], CAP, counts)
    upper = jnp.cumsum(counts, axis=1)
    lower = upper - counts
    ranks = jax.vmap(lambda subkey: jax.random.permutation(subkey, TOK_DEV))(jax.random.split(subkeys[2], block_count))
    ranks = ranks[:, :, None]
    inside = (ranks >= lower[:, None, :]) & (ranks < upper[:, None, :])
    window_id = jnp.sum(jnp.where(inside, jnp.arange(EXP_WIN)[None, None, :], 0), axis=2).reshape(TOKENS)
    routed = jnp.any(inside, axis=2).reshape(TOKENS)
    others = jax.vmap(lambda subkey: jax.random.permutation(subkey, EXPERTS_ALL - EXP_WIN)[:TOP])(jax.random.split(subkeys[3], TOKENS)) + EXP_WIN
    position = jax.random.randint(subkeys[4], (TOKENS, 1), 0, TOP)
    placed = routed[:, None] & (jnp.arange(TOP)[None, :] == position)
    return jnp.where(placed, window_id[:, None], others).astype(jnp.int32)


def steps_of(rng, extent, cuts, smallest, high):
    def one(dim, parts):
        draws = jax.random.uniform(jax.random.fold_in(jax.random.fold_in(rng, 6), dim), (parts,), jnp.float32, smallest / len(cuts), high / len(cuts))
        return jnp.repeat(jnp.exp(draws), extent[dim] // parts).reshape((-1,) + (1,) * (len(extent) - dim - 1))

    gain = one(*cuts[0])
    for cut in cuts[1:]:
        gain = gain * one(*cut)
    return gain


def scatter_about(stream_key, extent, scale, reach, pieces=(), held_as=jnp.bfloat16):
    drawn = jax.random.normal(stream_key, extent, jnp.float32) * scale
    if len(pieces) > 0:
        drawn = steps_of(stream_key, extent, pieces, -0.22, 0.18) * drawn
    return jnp.clip(drawn, min=-reach, max=reach).astype(held_as)


def setup_inputs(seed: int = 0, part: int = 0) -> dict:
    key_list = jax.random.split(jax.random.key(seed), 8)
    part_keys = jax.random.split(jax.random.fold_in(key_list[7], part), 8)
    tokens = scatter_about(part_keys[0], (TOKENS, D), 1.0, 6.0, ((0, 16),))
    grad_out = scatter_about(part_keys[1], (TOKENS, D), 1.0, 6.0, ((0, 16),))
    expert_ids = draw_expert_ids(jax.random.fold_in(jax.random.fold_in(key_list[7], part), 71), part)
    gate_weights = jnp.clip(0.05 + 0.55 * jax.random.uniform(part_keys[3], (TOKENS, TOP), jnp.float32) ** steps_of(part_keys[3], (TOKENS, TOP), ((0, 16),), -0.2, 0.2), 0.05, 0.6)
    w_gate = scatter_about(key_list[4], (EXP_WIN * I_WIN, D), D ** -0.5, 0.09375, ((0, 16),))
    w_up = scatter_about(key_list[5], (EXP_WIN * I_WIN, D), D ** -0.5, 0.09375, ((0, 16),))
    w_down = scatter_about(key_list[6], (EXP_WIN * I_WIN, D), I_WIN ** -0.5, 0.1875, ((0, 16),))
    return dict(tokens=tokens, grad_out=grad_out, expert_ids=expert_ids, gate_weights=gate_weights, w_gate=w_gate, w_up=w_up, w_down=w_down)


def reference(tokens, grad_out, expert_ids, gate_weights, w_gate, w_up, w_down):
    rows_max = (TOKENS // TOK_DEV) * CAP
    contract_last = (((1,), (1,)), ((), ()))
    contract_first = (((0,), (0,)), ((), ()))

    def expert_step(carry, expert):
        grad_acc, gate_acc = carry
        matches = expert_ids == expert
        member = jnp.any(matches, axis=1)
        gate_sum = jnp.sum(jnp.where(matches, gate_weights, jnp.float32(0.0)), axis=1)
        positions = jnp.nonzero(member, size=rows_max, fill_value=TOKENS)[0].astype(jnp.int32)
        occupied = positions < TOKENS
        clipped = jnp.minimum(positions, TOKENS - 1).astype(jnp.int32)
        rows_x = jnp.where(occupied[:, None], tokens[clipped], jnp.zeros((), tokens.dtype))
        rows_dy = jnp.where(occupied[:, None], grad_out[clipped], jnp.zeros((), grad_out.dtype))
        rows_gate = jnp.where(occupied, gate_sum[clipped], jnp.float32(0.0))
        start = (expert * I_WIN).astype(jnp.int32)
        gate_rows = lax.dynamic_slice_in_dim(w_gate, start, I_WIN, 0)
        up_rows = lax.dynamic_slice_in_dim(w_up, start, I_WIN, 0)
        down_rows = lax.dynamic_slice_in_dim(w_down, start, I_WIN, 0)
        pre_gate = lax.dot_general(rows_x, gate_rows, contract_last, preferred_element_type=jnp.float32)
        pre_up = lax.dot_general(rows_x, up_rows, contract_last, preferred_element_type=jnp.float32)
        sigmoid_gate = jax.nn.sigmoid(pre_gate)
        hidden = (pre_gate * sigmoid_gate * pre_up).astype(jnp.bfloat16)
        expert_out = jnp.dot(hidden, down_rows, preferred_element_type=jnp.float32)
        gate_dots = jnp.sum(rows_dy.astype(jnp.float32) * expert_out, axis=1)
        scaled = (rows_gate[:, None] * rows_dy.astype(jnp.float32)).astype(jnp.bfloat16)
        grad_hidden = lax.dot_general(scaled, down_rows, contract_last, preferred_element_type=jnp.float32)
        grad_pre_gate = (grad_hidden * pre_up * sigmoid_gate * (1.0 + pre_gate * (1.0 - sigmoid_gate))).astype(jnp.bfloat16)
        grad_pre_up = (grad_hidden * pre_gate * sigmoid_gate).astype(jnp.bfloat16)
        grad_down = lax.dot_general(hidden, scaled, contract_first, preferred_element_type=jnp.float32).astype(jnp.bfloat16)
        grad_gate_w = lax.dot_general(grad_pre_gate, rows_x, contract_first, preferred_element_type=jnp.float32).astype(jnp.bfloat16)
        grad_up_w = lax.dot_general(grad_pre_up, rows_x, contract_first, preferred_element_type=jnp.float32).astype(jnp.bfloat16)
        partial_dx = jnp.dot(grad_pre_gate, gate_rows, preferred_element_type=jnp.float32) + jnp.dot(grad_pre_up, up_rows, preferred_element_type=jnp.float32)
        grad_acc = grad_acc.at[positions].add(partial_dx, mode="drop")
        slot_hits = matches[clipped].astype(jnp.float32)
        gate_acc = gate_acc.at[positions].add(gate_dots[:, None] * slot_hits, mode="drop")
        return (grad_acc, gate_acc), (grad_gate_w, grad_up_w, grad_down)

    start_carry = (jnp.zeros((TOKENS, D), jnp.float32), jnp.zeros((TOKENS, TOP), jnp.float32))
    (grad_acc, gate_acc), (stack_gate, stack_up, stack_down) = lax.scan(expert_step, start_carry, jnp.arange(EXP_WIN, dtype=jnp.int32))
    grad_tokens = grad_acc.astype(jnp.bfloat16)
    return (grad_tokens, gate_acc, stack_gate.reshape(EXP_WIN * I_WIN, D), stack_up.reshape(EXP_WIN * I_WIN, D), stack_down.reshape(EXP_WIN * I_WIN, D))
```

```python
import functools

import jax
import jax.numpy as jnp
from jax import lax
from jax.experimental import pallas as pl
from jax.experimental.pallas import tpu as pltpu
from jax.sharding import PartitionSpec as P

SPAN = 8
CAP = 6
ROWS = 16
LANE = 128
FIRST = (((0,), (0,)), ((), ()))
LAST = (((1,), (1,)), ((), ()))
F32 = jnp.float32
BF16 = jnp.bfloat16


def loop(count, body):
    if count <= 2:
        for i in range(count):
            body(i)
    else:
        pl.loop(0, count)(body)


def exchange_kernel(
    experts,
    tokens_ref, grad_ref, ids_ref, gates_ref, wg_ref, wu_ref, wd_ref,
    buf, act_ref, sel_ref, fin,
    tok_v, dy_v, w_v, send, dxb, rc, r2, r1,
    in_sem, s1_s, s1_r, a1_s, a1_r, a2_s, a2_r, a3_s, a3_r, ac_s, ac_r,
    rc_s, rc_r, r2_s, r2_r, r1_s, r1_r, r0_s, r0_r,
):
    features = tok_v.shape[1]
    half = features // 2
    hid = wg_ref.shape[0]
    dp = lax.axis_index("dp")
    flat = lax.axis_index("expert") * 2 + dp
    octet = flat // SPAN
    pos = flat % SPAN
    bit1 = (pos // 2) % 2
    bit2 = pos // 4
    step2 = 2 - 4 * bit1
    step4 = 4 - 8 * bit2
    step_c = 1 - 2 * dp
    first = jnp.where(dp == 0, step4, step2)
    second = jnp.where(dp == 0, step2, step4)

    def dev(index):
        return {"expert": index // 2, "dp": index % 2}

    barrier = pltpu.get_barrier_semaphore()
    for step in (first, second, step_c):
        pl.semaphore_signal(barrier, 1, device_id=dev(flat + step), device_id_type=pl.DeviceIdType.MESH)

    def greet(i):
        other = lax.rem(octet + i + 1, experts) * SPAN + pos
        pl.semaphore_signal(barrier, 1, device_id=dev(other), device_id_type=pl.DeviceIdType.MESH)

    loop(experts - 1, greet)

    loads = [
        pltpu.make_async_copy(tokens_ref, tok_v, in_sem.at[0]),
        pltpu.make_async_copy(grad_ref, dy_v, in_sem.at[1]),
        pltpu.make_async_copy(wg_ref, w_v.at[pl.ds(0, hid)], in_sem.at[2]),
        pltpu.make_async_copy(wu_ref, w_v.at[pl.ds(hid, hid)], in_sem.at[3]),
        pltpu.make_async_copy(wd_ref, w_v.at[pl.ds(2 * hid, hid)], in_sem.at[4]),
    ]
    for copy in loads:
        copy.start()

    count = ids_ref.shape[0]
    width = experts * ROWS
    lane = lax.broadcasted_iota(jnp.int32, (count, width), 1)
    lane_expert = lane // ROWS
    lane_row = lane % 8
    lane_dy = (lane // 8) % 2
    member = jnp.zeros((count, width), F32)
    gate = jnp.zeros((count, width), F32)
    for s in range(ids_ref.shape[1]):
        hit = ids_ref[:, s : s + 1] == lane_expert
        member = member + jnp.where(hit, 1.0, 0.0)
        gate = gate + jnp.where(hit, gates_ref[:, s : s + 1], 0.0)
    lower = jnp.where(
        lax.broadcasted_iota(jnp.int32, (count, count), 0)
        >= lax.broadcasted_iota(jnp.int32, (count, count), 1),
        1.0, 0.0,
    ).astype(BF16)
    rank = jnp.dot(lower, member.astype(BF16), preferred_element_type=F32)
    chosen = jnp.where(
        (member > 0.5) & (rank == (lane_row + 1).astype(F32)) & (lane_row < CAP), 1.0, 0.0
    )
    sel_x = jnp.where(lane_dy == 0, chosen, 0.0)
    sel_dy = jnp.where(lane_dy == 1, chosen, 0.0)
    gate_hi = gate.astype(BF16).astype(F32)
    gate_mix = (sel_x * gate_hi + sel_dy * (gate - gate_hi)).astype(BF16)
    sel_x = sel_x.astype(BF16)
    sel_dy = sel_dy.astype(BF16)
    sel_ref[0] = sel_x
    sel_ref[1] = sel_dy
    send[:, :, features:] = (
        lax.dot_general(gate_mix, jnp.ones((count, LANE), BF16), FIRST, preferred_element_type=F32)
        .astype(BF16)
        .reshape(experts, ROWS, LANE)
    )
    loads[0].wait()
    loads[1].wait()
    tile = features // 4
    for c in range(4):
        cols = pl.ds(c * tile, tile)
        block = lax.dot_general(
            sel_x, tok_v[:, cols], FIRST, preferred_element_type=F32
        ) + lax.dot_general(sel_dy, dy_v[:, cols], FIRST, preferred_element_type=F32)
        send[:, :, cols] = block.astype(BF16).reshape(experts, ROWS, tile)
    buf[flat] = send[octet]
    pl.semaphore_wait(barrier, 3 + experts - 1)

    def remote(src, dst, ssem, rsem, index):
        return pltpu.make_async_remote_copy(
            src_ref=src, dst_ref=dst, send_sem=ssem, recv_sem=rsem,
            device_id=dev(index), device_id_type=pl.DeviceIdType.MESH,
        )

    def source(d):
        return lax.rem(octet - d + experts, experts)

    def s1(i):
        other = lax.rem(octet + i + 1, experts)
        return remote(send.at[other], buf.at[flat], s1_s.at[i], s1_r.at[i], other * SPAN + pos)

    def pass_on(slot, ssem, rsem, index):
        return remote(buf.at[slot], buf.at[slot], ssem, rsem, index)

    def base(d):
        return source(d) * SPAN + pos

    def a1(d):
        return pass_on(base(d), a1_s.at[d], a1_r.at[d], flat + first)

    def a2(d):
        return pass_on(base(d), a2_s.at[d], a2_r.at[d], flat + second)

    def a3(d):
        return pass_on(base(d) + first, a3_s.at[d], a3_r.at[d], flat + second)

    offsets = (0, first, second, first + second)

    def ac(d, k):
        return pass_on(base(d) + offsets[k], ac_s.at[d, k], ac_r.at[d, k], flat + step_c)

    def own(d):
        a1(d).start()
        a2(d).start()
        ac(d, 0).start()

    loop(experts - 1, lambda i: s1(i).start())
    own(0)

    def after_s1(i):
        s1(i).wait_recv()
        own(i + 1)

    def after_a1(d):
        a1(d).wait_recv()
        a3(d).start()
        ac(d, 1).start()

    def after_a2(d):
        a2(d).wait_recv()
        ac(d, 2).start()

    def after_a3(d):
        a3(d).wait_recv()
        ac(d, 3).start()

    after_a1(0)
    after_a2(0)
    loop(experts - 1, after_s1)
    after_a3(0)

    def rest(i):
        after_a1(i + 1)
        after_a2(i + 1)

    loop(experts - 1, rest)
    loop(experts - 1, lambda i: after_a3(i + 1))
    for copy in loads[2:]:
        copy.wait()

    def all_core(d):
        for k in range(4):
            ac(d, k).wait_recv()

    loop(experts, all_core)

    def compute(f):
        rows = pl.ds(f * SPAN, SPAN)
        total = jnp.zeros((SPAN * ROWS, 3 * hid), F32)
        for c in range(4):
            cols = pl.ds(c * tile, tile)
            total = total + lax.dot_general(
                buf[rows, :, cols].reshape(SPAN * ROWS, tile), w_v[:, cols], LAST,
                preferred_element_type=F32,
            )
        total = total.reshape(SPAN, 2, 8, 3 * hid)
        from_x = total[:, 0].reshape(SPAN * 8, 3 * hid)
        from_dy = total[:, 1].reshape(SPAN * 8, 3 * hid)
        pre_gate = from_x[:, :hid]
        pre_up = from_x[:, hid : 2 * hid]
        back = from_dy[:, 2 * hid :]
        packed = buf[rows, :, pl.ds(features, LANE)].astype(F32)
        weight = (packed[:, :8] + packed[:, 8:]).reshape(SPAN * 8, LANE)
        sig = jax.nn.sigmoid(pre_gate)
        silu = pre_gate * sig
        hidden = silu * pre_up
        dots = jnp.sum(hidden.astype(BF16).astype(F32) * back, axis=1, keepdims=True)
        grad_hidden = back * weight
        grad_gate = grad_hidden * pre_up * sig * (1.0 + pre_gate * (1.0 - sig))
        grad_up = grad_hidden * silu
        down = (hidden * weight).reshape(SPAN, 8, hid)
        none = jnp.zeros((SPAN, 8, hid), F32)
        upper = jnp.concatenate([grad_gate.reshape(SPAN, 8, hid), grad_up.reshape(SPAN, 8, hid), none], axis=2)
        under = jnp.concatenate([none, none, down], axis=2)
        act_ref[rows] = jnp.concatenate([upper, under], axis=1).astype(BF16)
        pair = jnp.concatenate([grad_gate, grad_up], axis=1).astype(BF16)
        spread = jnp.broadcast_to(dots, (SPAN * 8, LANE)).reshape(SPAN, 8, LANE)
        dxb[rows, :, pl.ds(half, LANE)] = jnp.concatenate([spread, spread], axis=1).astype(BF16)
        step = half // 2
        for c in range(2):
            left = jnp.dot(pair, w_v[: 2 * hid, c * step : (c + 1) * step], preferred_element_type=F32)
            right = jnp.dot(
                pair, w_v[: 2 * hid, half + c * step : half + (c + 1) * step], preferred_element_type=F32
            )
            dxb[rows, :, pl.ds(c * step, step)] = jnp.concatenate(
                [left.reshape(SPAN, 8, step), right.reshape(SPAN, 8, step)], axis=1
            ).astype(BF16)

    loop(experts, compute)

    partner_offsets = (0, second, first, first + second)

    def back_core(d, k):
        return remote(
            dxb.at[base(d) + step_c + partner_offsets[k]], rc.at[d, k], rc_s.at[d, k], rc_r.at[d, k], flat + step_c
        )

    def back_second(d, k):
        return remote(
            dxb.at[base(d) + second + (0, first)[k]], r2.at[d, k], r2_s.at[d, k], r2_r.at[d, k], flat + second
        )

    def back_first(d):
        return remote(dxb.at[base(d) + first], r1.at[d], r1_s.at[d], r1_r.at[d], flat + first)

    def home(i):
        to = source(i + 1)
        return remote(dxb.at[base(i + 1)], fin.at[octet], r0_s.at[i], r0_r.at[i], to * SPAN + pos)

    def add(slot, piece):
        dxb[slot] = (dxb[slot].astype(F32) + piece.astype(F32)).astype(BF16)

    def start_core(i):
        d = experts - 1 - i
        for k in (2, 3, 1, 0):
            back_core(d, k).start()

    loop(experts, start_core)

    def sum_core(i):
        d = experts - 1 - i
        for k in (2, 3):
            back_core(d, k).wait_recv()
            add(base(d) + offsets[k], rc[d, k])
            back_second(d, k - 2).start()
        for k in (1, 0):
            back_core(d, k).wait_recv()
            add(base(d) + offsets[k], rc[d, k])

    loop(experts, sum_core)

    def sum_second(i):
        d = experts - 1 - i
        back_second(d, 1).wait_recv()
        add(base(d) + first, r2[d, 1])
        back_first(d).start()
        back_second(d, 0).wait_recv()
        add(base(d), r2[d, 0])

    loop(experts, sum_second)

    def sum_first(i):
        d = experts - 1 - i
        back_first(d).wait_recv()
        add(base(d), r1[d])
        home(d - 1).start()

    loop(experts - 1, sum_first)
    back_first(0).wait_recv()
    fin[octet] = (dxb[flat].astype(F32) + r1[0].astype(F32)).astype(BF16)
    loop(experts - 1, lambda i: home(i).wait_recv())

    def finish(d):
        a1(d).wait_send()
        a2(d).wait_send()
        a3(d).wait_send()
        back_first(d).wait_send()
        for k in range(4):
            ac(d, k).wait_send()
            back_core(d, k).wait_send()
        for k in range(2):
            back_second(d, k).wait_send()

    loop(experts, finish)

    def finish_far(i):
        s1(i).wait_send()
        home(i).wait_send()

    loop(experts - 1, finish_far)


def output_kernel(
    experts, buf_ref, act_ref, sel_ref, fin_ref, dots_ref, ids_ref,
    gt_ref, gg_ref, wg_ref, wu_ref, wd_ref,
):
    hid = wg_ref.shape[0]
    grads = lax.dot_general(act_ref[...], buf_ref[...], FIRST, preferred_element_type=F32)
    wg_ref[...] = grads[:hid].astype(BF16)
    wu_ref[...] = grads[hid : 2 * hid].astype(BF16)
    wd_ref[...] = grads[2 * hid :].astype(BF16)
    gt_ref[...] = jnp.dot(sel_ref[0], fin_ref[...], preferred_element_type=F32).astype(BF16)

    @pl.when(pl.program_id(0) == 0)
    def _():
        dots = jnp.dot(sel_ref[0], dots_ref[...], preferred_element_type=F32)
        gg_ref[...] = jnp.where(ids_ref[...] < experts, dots[:, : ids_ref.shape[1]], 0.0)


def local(tokens, grad_out, expert_ids, gate_weights, w_gate, w_up, w_down):
    flat_count = lax.axis_size(("expert", "dp"))
    experts = flat_count // SPAN
    count, features = tokens.shape
    hid = w_gate.shape[0]
    half = features // 2
    wide = features + LANE
    narrow = half + LANE
    slots = experts * SPAN
    far = max(experts - 1, 1)
    vmem = pl.BlockSpec(memory_space=pltpu.VMEM)
    anyspace = pl.BlockSpec(memory_space=pl.ANY)
    sem = pltpu.SemaphoreType.DMA
    buf, act, sel, fin = pl.pallas_call(
        functools.partial(exchange_kernel, experts),
        out_shape=(
            jax.ShapeDtypeStruct((slots, ROWS, wide), BF16),
            jax.ShapeDtypeStruct((slots, ROWS, 3 * hid), BF16),
            jax.ShapeDtypeStruct((2, count, experts * ROWS), BF16),
            jax.ShapeDtypeStruct((experts, ROWS, narrow), BF16),
        ),
        in_specs=[anyspace, anyspace, vmem, vmem, anyspace, anyspace, anyspace],
        out_specs=(vmem, vmem, vmem, vmem),
        scratch_shapes=[
            pltpu.VMEM((count, features), BF16),
            pltpu.VMEM((count, features), BF16),
            pltpu.VMEM((3 * hid, features), BF16),
            pltpu.VMEM((experts, ROWS, wide), BF16),
            pltpu.VMEM((slots, ROWS, narrow), BF16),
            pltpu.VMEM((experts, 4, ROWS, narrow), BF16),
            pltpu.VMEM((experts, 2, ROWS, narrow), BF16),
            pltpu.VMEM((experts, ROWS, narrow), BF16),
            sem((5,)),
            sem((far,)), sem((far,)),
            sem((experts,)), sem((experts,)),
            sem((experts,)), sem((experts,)),
            sem((experts,)), sem((experts,)),
            sem((experts, 4)), sem((experts, 4)),
            sem((experts, 4)), sem((experts, 4)),
            sem((experts, 2)), sem((experts, 2)),
            sem((experts,)), sem((experts,)),
            sem((far,)), sem((far,)),
        ],
        compiler_params=pltpu.CompilerParams(
            collective_id=0, has_side_effects=True, vmem_limit_bytes=56 * 1024 * 1024
        ),
    )(tokens, grad_out, expert_ids, gate_weights, w_gate, w_up, w_down)

    tiles = 4
    tile = features // tiles
    rows = slots * ROWS
    deep = experts * ROWS
    fin2 = fin.reshape(deep, narrow)
    wide_out = pl.BlockSpec((hid, tile), lambda t: (0, t))
    return pl.pallas_call(
        functools.partial(output_kernel, experts),
        grid=(tiles,),
        out_shape=(
            jax.ShapeDtypeStruct((count, features), BF16),
            jax.ShapeDtypeStruct(gate_weights.shape, F32),
            jax.ShapeDtypeStruct((hid, features), BF16),
            jax.ShapeDtypeStruct((hid, features), BF16),
            jax.ShapeDtypeStruct((hid, features), BF16),
        ),
        in_specs=[
            pl.BlockSpec((rows, tile), lambda t: (0, t)),
            pl.BlockSpec((rows, 3 * hid), lambda t: (0, 0)),
            pl.BlockSpec((1, count, deep), lambda t: (t // 2, 0, 0)),
            pl.BlockSpec((deep, tile), lambda t: (0, t % 2)),
            pl.BlockSpec((deep, LANE), lambda t: (0, half // LANE)),
            pl.BlockSpec(expert_ids.shape, lambda t: (0, 0)),
        ],
        out_specs=(
            pl.BlockSpec((count, tile), lambda t: (0, t)),
            pl.BlockSpec(gate_weights.shape, lambda t: (0, 0)),
            wide_out, wide_out, wide_out,
        ),
        compiler_params=pltpu.CompilerParams(vmem_limit_bytes=40 * 1024 * 1024),
    )(buf.reshape(rows, wide), act.reshape(rows, 3 * hid), sel, fin2, fin2, expert_ids)


def solution(mesh):
    rows = P(("groups", "expert", "dp"), None)
    weights = P(("expert", "dp"), None)
    return jax.shard_map(
        local,
        mesh=mesh,
        in_specs=(rows,) * 4 + (weights,) * 3,
        out_specs=(rows,) * 5,
        check_vma=False,
    )
```

```python
import functools

import jax
import jax.numpy as jnp
from jax import lax
from jax.experimental import pallas as pl
from jax.experimental.pallas import tpu as pltpu
from jax.sharding import PartitionSpec as P

SPAN = 8
CAP = 6
ROWS = 16
LANE = 128
FIRST = (((0,), (0,)), ((), ()))
LAST = (((1,), (1,)), ((), ()))
F32 = jnp.float32
BF16 = jnp.bfloat16


def loop(count, body):
    if count <= 2:
        for i in range(count):
            body(i)
    else:
        pl.loop(0, count)(body)


def exchange_kernel(
    experts,
    tokens_ref, grad_ref, ids_ref, gates_ref, wg_ref, wu_ref, wd_ref,
    buf_out, tail_out, act_out, sel_ref, fin,
    tok_v, dy_v, w_v, send, buf, tail, act, dxb, rc, r2, r1,
    in_sem, out_sem, s1_s, s1_r, a1_s, a1_r, a2_s, a2_r, a3_s, a3_r, ac_s, ac_r,
    rc_s, rc_r, r2_s, r2_r, r1_s, r1_r, r0_s, r0_r,
):
    features = tok_v.shape[1]
    half = features // 2
    hid = wg_ref.shape[0]
    dp = lax.axis_index("dp")
    flat = lax.axis_index("expert") * 2 + dp
    octet = flat // SPAN
    pos = flat % SPAN
    bit1 = (pos // 2) % 2
    bit2 = pos // 4
    step2 = 2 - 4 * bit1
    step4 = 4 - 8 * bit2
    step_c = 1 - 2 * dp
    first = jnp.where(dp == 0, step4, step2)
    second = jnp.where(dp == 0, step2, step4)

    def dev(index):
        return {"expert": index // 2, "dp": index % 2}

    barrier = pltpu.get_barrier_semaphore()
    for step in (first, second, step_c):
        pl.semaphore_signal(barrier, 1, device_id=dev(flat + step), device_id_type=pl.DeviceIdType.MESH)

    def greet(i):
        other = lax.rem(octet + i + 1, experts) * SPAN + pos
        pl.semaphore_signal(barrier, 1, device_id=dev(other), device_id_type=pl.DeviceIdType.MESH)

    loop(experts - 1, greet)

    loads = [
        pltpu.make_async_copy(tokens_ref, tok_v, in_sem.at[0]),
        pltpu.make_async_copy(grad_ref, dy_v, in_sem.at[1]),
        pltpu.make_async_copy(wg_ref, w_v.at[pl.ds(0, hid)], in_sem.at[2]),
        pltpu.make_async_copy(wu_ref, w_v.at[pl.ds(hid, hid)], in_sem.at[3]),
        pltpu.make_async_copy(wd_ref, w_v.at[pl.ds(2 * hid, hid)], in_sem.at[4]),
    ]
    for copy in loads:
        copy.start()

    count = ids_ref.shape[1]
    deep = experts * ROWS
    row = lax.broadcasted_iota(jnp.int32, (deep, count), 0)
    row_expert = row // ROWS
    row_slot = row % 8
    row_dy = (row // 8) % 2
    member = jnp.zeros((deep, count), F32)
    gate = jnp.zeros((deep, count), F32)
    for s in range(ids_ref.shape[0]):
        hit = ids_ref[s : s + 1, :] == row_expert
        member = member + jnp.where(hit, 1.0, 0.0)
        gate = gate + jnp.where(hit, gates_ref[s : s + 1, :], 0.0)
    upper = jnp.where(
        lax.broadcasted_iota(jnp.int32, (count, count), 0)
        <= lax.broadcasted_iota(jnp.int32, (count, count), 1),
        1.0, 0.0,
    ).astype(BF16)
    rank = jnp.dot(member.astype(BF16), upper, preferred_element_type=F32)

    def choose(wanted):
        chosen = jnp.where((member > 0.5) & (rank == wanted.astype(F32)), 1.0, 0.0)
        return (
            chosen,
            jnp.where(row_dy == 0, chosen, 0.0).astype(BF16),
            jnp.where(row_dy == 1, chosen, 0.0).astype(BF16),
        )

    chosen, sel_x, sel_dy = choose(jnp.where(row_slot < CAP, row_slot + 1, -1))
    weight = jnp.sum(chosen * gate, axis=1, keepdims=True)
    weight_hi = weight.astype(BF16).astype(F32)
    row_gate = jnp.where(row_dy == 0, weight_hi, weight - weight_hi)
    sel_ref[0] = sel_x
    sel_ref[1] = sel_dy
    tile = features // 4
    main = 3 * tile
    send[:, :, main:] = jnp.broadcast_to(row_gate[:, :1], (deep, LANE)).astype(BF16).reshape(experts, ROWS, LANE)
    loads[0].wait()
    loads[1].wait()
    for c in range(3):
        cols = pl.ds(c * tile, tile)
        _, end_x, end_dy = choose(jnp.where(row_slot < CAP, -1, (row_slot - CAP) * 3 + c + 1))
        block = (
            jnp.dot(sel_x, tok_v[:, cols], preferred_element_type=F32)
            + jnp.dot(sel_dy, dy_v[:, cols], preferred_element_type=F32)
            + jnp.dot(end_x, tok_v[:, main:], preferred_element_type=F32)
            + jnp.dot(end_dy, dy_v[:, main:], preferred_element_type=F32)
        )
        send[:, :, cols] = block.astype(BF16).reshape(experts, ROWS, tile)
    buf[flat] = send[octet]
    pl.semaphore_wait(barrier, 3 + experts - 1)

    def remote(src, dst, ssem, rsem, index):
        return pltpu.make_async_remote_copy(
            src_ref=src, dst_ref=dst, send_sem=ssem, recv_sem=rsem,
            device_id=dev(index), device_id_type=pl.DeviceIdType.MESH,
        )

    def source(d):
        return lax.rem(octet - d + experts, experts)

    def s1(i):
        other = lax.rem(octet + i + 1, experts)
        return remote(send.at[other], buf.at[flat], s1_s.at[i], s1_r.at[i], other * SPAN + pos)

    def pass_on(slot, ssem, rsem, index):
        return remote(buf.at[slot], buf.at[slot], ssem, rsem, index)

    def base(d):
        return source(d) * SPAN + pos

    def a1(d):
        return pass_on(base(d), a1_s.at[d], a1_r.at[d], flat + first)

    def a2(d):
        return pass_on(base(d), a2_s.at[d], a2_r.at[d], flat + second)

    def a3(d):
        return pass_on(base(d) + first, a3_s.at[d], a3_r.at[d], flat + second)

    offsets = (0, first, second, first + second)

    def ac(d, k):
        return pass_on(base(d) + offsets[k], ac_s.at[d, k], ac_r.at[d, k], flat + step_c)

    def own(d):
        a1(d).start()
        a2(d).start()
        ac(d, 0).start()

    loop(experts - 1, lambda i: s1(i).start())
    own(0)

    def after_s1(i):
        s1(i).wait_recv()
        own(i + 1)

    def after_a1(d):
        a1(d).wait_recv()
        a3(d).start()
        ac(d, 1).start()

    def after_a2(d):
        a2(d).wait_recv()
        ac(d, 2).start()

    def after_a3(d):
        a3(d).wait_recv()
        ac(d, 3).start()

    after_a1(0)
    after_a2(0)
    loop(experts - 1, after_s1)
    after_a3(0)

    def rest(i):
        after_a1(i + 1)
        after_a2(i + 1)

    loop(experts - 1, rest)
    for copy in loads[2:]:
        copy.wait()

    deep_f = SPAN * ROWS
    to_row = lax.broadcasted_iota(jnp.int32, (deep_f, deep_f), 0)
    from_row = lax.broadcasted_iota(jnp.int32, (deep_f, deep_f), 1)
    to_slot = to_row % 8
    kept = (to_slot < CAP) & (from_row == (to_row // 8) * 8 + CAP + to_slot // 3)

    def compute(d):
        for k in range(4):
            ac(d, k).wait_recv()
        rows = pl.ds(source(d) * SPAN, SPAN)
        total = jnp.zeros((deep_f, 3 * hid), F32)
        ends = jnp.zeros((deep_f, tile), F32)
        for c in range(3):
            cols = pl.ds(c * tile, tile)
            piece = buf[rows, :, cols].reshape(deep_f, tile)
            total = total + lax.dot_general(piece, w_v[:, cols], LAST, preferred_element_type=F32)
            move = jnp.where(kept & (to_slot % 3 == c), 1.0, 0.0).astype(BF16)
            ends = ends + jnp.dot(move, piece, preferred_element_type=F32)
        ends = ends.astype(BF16)
        tail[rows] = ends.reshape(SPAN, ROWS, tile)
        total = total + lax.dot_general(ends, w_v[:, main:], LAST, preferred_element_type=F32)
        total = total.reshape(SPAN, 2, 8, 3 * hid)
        from_x = total[:, 0].reshape(SPAN * 8, 3 * hid)
        from_dy = total[:, 1].reshape(SPAN * 8, 3 * hid)
        pre_gate = from_x[:, :hid]
        pre_up = from_x[:, hid : 2 * hid]
        back = from_dy[:, 2 * hid :]
        packed = buf[rows, :, pl.ds(main, LANE)].astype(F32)
        weight = (packed[:, :8] + packed[:, 8:]).reshape(SPAN * 8, LANE)
        sig = jax.nn.sigmoid(pre_gate)
        silu = pre_gate * sig
        hidden = silu * pre_up
        dots = jnp.sum(hidden.astype(BF16).astype(F32) * back, axis=1, keepdims=True)
        grad_hidden = back * weight
        grad_gate = grad_hidden * pre_up * sig * (1.0 + pre_gate * (1.0 - sig))
        grad_up = grad_hidden * silu
        down = (hidden * weight).reshape(SPAN, 8, hid)
        none = jnp.zeros((SPAN, 8, hid), F32)
        upper = jnp.concatenate([grad_gate.reshape(SPAN, 8, hid), grad_up.reshape(SPAN, 8, hid), none], axis=2)
        under = jnp.concatenate([none, none, down], axis=2)
        act[rows] = jnp.concatenate([upper, under], axis=1).astype(BF16)
        pair = jnp.concatenate([grad_gate, grad_up], axis=1).astype(BF16)
        spread = jnp.broadcast_to(dots, (SPAN * 8, LANE)).reshape(SPAN, 8, LANE)
        dxb[rows, :, pl.ds(half, LANE)] = jnp.concatenate([spread, spread], axis=1).astype(BF16)
        step = half // 2
        for c in range(2):
            left = jnp.dot(pair, w_v[: 2 * hid, c * step : (c + 1) * step], preferred_element_type=F32)
            right = jnp.dot(
                pair, w_v[: 2 * hid, half + c * step : half + (c + 1) * step], preferred_element_type=F32
            )
            dxb[rows, :, pl.ds(c * step, step)] = jnp.concatenate(
                [left.reshape(SPAN, 8, step), right.reshape(SPAN, 8, step)], axis=1
            ).astype(BF16)


    partner_offsets = (0, second, first, first + second)

    def back_core(d, k):
        return remote(
            dxb.at[base(d) + step_c + partner_offsets[k]], rc.at[d, k], rc_s.at[d, k], rc_r.at[d, k], flat + step_c
        )

    def back_second(d, k):
        return remote(
            dxb.at[base(d) + second + (0, first)[k]], r2.at[d, k], r2_s.at[d, k], r2_r.at[d, k], flat + second
        )

    def back_first(d):
        return remote(dxb.at[base(d) + first], r1.at[d], r1_s.at[d], r1_r.at[d], flat + first)

    def home(i):
        to = source(i + 1)
        return remote(dxb.at[base(i + 1)], fin.at[octet], r0_s.at[i], r0_r.at[i], to * SPAN + pos)

    def add(slot, piece):
        dxb[slot] = (dxb[slot].astype(F32) + piece.astype(F32)).astype(BF16)

    def start_core(d):
        for k in (2, 3, 1, 0):
            back_core(d, k).start()

    compute(0)
    start_core(0)

    def far_compute(i):
        after_a3(i + 1)
        compute(i + 1)
        start_core(i + 1)

    loop(experts - 1, far_compute)
    stores = [
        pltpu.make_async_copy(buf, buf_out, out_sem.at[0]),
        pltpu.make_async_copy(tail, tail_out, out_sem.at[1]),
        pltpu.make_async_copy(act, act_out, out_sem.at[2]),
    ]
    for copy in stores:
        copy.start()

    def sum_core(d):
        for k in (2, 3):
            back_core(d, k).wait_recv()
            add(base(d) + offsets[k], rc[d, k])
            back_second(d, k - 2).start()
        for k in (1, 0):
            back_core(d, k).wait_recv()
            add(base(d) + offsets[k], rc[d, k])

    loop(experts, sum_core)

    def sum_second(d):
        back_second(d, 1).wait_recv()
        add(base(d) + first, r2[d, 1])
        back_first(d).start()
        back_second(d, 0).wait_recv()
        add(base(d), r2[d, 0])

    loop(experts, sum_second)

    def sum_first(i):
        d = i + 1
        back_first(d).wait_recv()
        add(base(d), r1[d])
        home(d - 1).start()

    loop(experts - 1, sum_first)
    back_first(0).wait_recv()
    fin[octet] = (dxb[flat].astype(F32) + r1[0].astype(F32)).astype(BF16)
    loop(experts - 1, lambda i: home(i).wait_recv())

    def finish(d):
        a1(d).wait_send()
        a2(d).wait_send()
        a3(d).wait_send()
        back_first(d).wait_send()
        for k in range(4):
            ac(d, k).wait_send()
            back_core(d, k).wait_send()
        for k in range(2):
            back_second(d, k).wait_send()

    loop(experts, finish)

    def finish_far(i):
        s1(i).wait_send()
        home(i).wait_send()

    loop(experts - 1, finish_far)
    for copy in stores:
        copy.wait()


def output_kernel(
    experts, buf_ref, tail_ref, act_ref, sel_ref, fin_ref, dots_ref, ids_ref,
    gt_ref, gg_ref, wg_ref, wu_ref, wd_ref,
):
    hid = wg_ref.shape[0]
    step = pl.program_id(0)

    def weights(rows):
        grads = lax.dot_general(act_ref[...], rows, FIRST, preferred_element_type=F32)
        wg_ref[...] = grads[:hid].astype(BF16)
        wu_ref[...] = grads[hid : 2 * hid].astype(BF16)
        wd_ref[...] = grads[2 * hid :].astype(BF16)

    @pl.when(step < 3)
    def _():
        weights(buf_ref[...])

    @pl.when(step == 3)
    def _():
        weights(tail_ref[...])

    gt_ref[...] = lax.dot_general(sel_ref[0], fin_ref[...], FIRST, preferred_element_type=F32).astype(BF16)

    @pl.when(step == 0)
    def _():
        dots = lax.dot_general(dots_ref[...], sel_ref[0], FIRST, preferred_element_type=F32)
        gg_ref[...] = jnp.where(ids_ref[...] < experts, dots[: ids_ref.shape[0]], 0.0)


def local(tokens, grad_out, expert_ids, gate_weights, w_gate, w_up, w_down):
    flat_count = lax.axis_size(("expert", "dp"))
    experts = flat_count // SPAN
    count, features = tokens.shape
    hid = w_gate.shape[0]
    half = features // 2
    tiles = 4
    tile = features // tiles
    wide = 3 * tile + LANE
    deep = experts * ROWS
    ids_t, gates_t = expert_ids.T, gate_weights.T
    narrow = half + LANE
    slots = experts * SPAN
    far = max(experts - 1, 1)
    vmem = pl.BlockSpec(memory_space=pltpu.VMEM)
    anyspace = pl.BlockSpec(memory_space=pl.ANY)
    sem = pltpu.SemaphoreType.DMA
    buf, tail, act, sel, fin = pl.pallas_call(
        functools.partial(exchange_kernel, experts),
        out_shape=(
            jax.ShapeDtypeStruct((slots, ROWS, wide), BF16),
            jax.ShapeDtypeStruct((slots, ROWS, tile), BF16),
            jax.ShapeDtypeStruct((slots, ROWS, 3 * hid), BF16),
            jax.ShapeDtypeStruct((2, deep, count), BF16),
            jax.ShapeDtypeStruct((experts, ROWS, narrow), BF16),
        ),
        in_specs=[anyspace, anyspace, vmem, vmem, anyspace, anyspace, anyspace],
        out_specs=(anyspace, anyspace, anyspace, vmem, vmem),
        scratch_shapes=[
            pltpu.VMEM((count, features), BF16),
            pltpu.VMEM((count, features), BF16),
            pltpu.VMEM((3 * hid, features), BF16),
            pltpu.VMEM((experts, ROWS, wide), BF16),
            pltpu.VMEM((slots, ROWS, wide), BF16),
            pltpu.VMEM((slots, ROWS, tile), BF16),
            pltpu.VMEM((slots, ROWS, 3 * hid), BF16),
            pltpu.VMEM((slots, ROWS, narrow), BF16),
            pltpu.VMEM((experts, 4, ROWS, narrow), BF16),
            pltpu.VMEM((experts, 2, ROWS, narrow), BF16),
            pltpu.VMEM((experts, ROWS, narrow), BF16),
            sem((5,)), sem((3,)),
            sem((far,)), sem((far,)),
            sem((experts,)), sem((experts,)),
            sem((experts,)), sem((experts,)),
            sem((experts,)), sem((experts,)),
            sem((experts, 4)), sem((experts, 4)),
            sem((experts, 4)), sem((experts, 4)),
            sem((experts, 2)), sem((experts, 2)),
            sem((experts,)), sem((experts,)),
            sem((far,)), sem((far,)),
        ],
        compiler_params=pltpu.CompilerParams(
            collective_id=0, has_side_effects=True, vmem_limit_bytes=56 * 1024 * 1024
        ),
    )(tokens, grad_out, ids_t, gates_t, w_gate, w_up, w_down)

    rows = slots * ROWS
    fin2 = fin.reshape(deep, narrow)
    wide_out = pl.BlockSpec((hid, tile), lambda t: (0, t))
    grad_tokens, grad_gates, grad_gate, grad_up, grad_down = pl.pallas_call(
        functools.partial(output_kernel, experts),
        grid=(tiles,),
        out_shape=(
            jax.ShapeDtypeStruct((count, features), BF16),
            jax.ShapeDtypeStruct(gates_t.shape, F32),
            jax.ShapeDtypeStruct((hid, features), BF16),
            jax.ShapeDtypeStruct((hid, features), BF16),
            jax.ShapeDtypeStruct((hid, features), BF16),
        ),
        in_specs=[
            pl.BlockSpec((rows, tile), lambda t: (0, jnp.minimum(t, 2))),
            pl.BlockSpec((rows, tile), lambda t: (0, 0)),
            pl.BlockSpec((rows, 3 * hid), lambda t: (0, 0)),
            pl.BlockSpec((1, deep, count), lambda t: (t // 2, 0, 0)),
            pl.BlockSpec((deep, tile), lambda t: (0, t % 2)),
            pl.BlockSpec((deep, LANE), lambda t: (0, half // LANE)),
            pl.BlockSpec(ids_t.shape, lambda t: (0, 0)),
        ],
        out_specs=(
            pl.BlockSpec((count, tile), lambda t: (0, t)),
            pl.BlockSpec(gates_t.shape, lambda t: (0, 0)),
            wide_out, wide_out, wide_out,
        ),
        compiler_params=pltpu.CompilerParams(vmem_limit_bytes=60 * 1024 * 1024),
    )(buf.reshape(rows, wide), tail.reshape(rows, tile), act.reshape(rows, 3 * hid), sel, fin2, fin2, ids_t)
    return grad_tokens, grad_gates.T, grad_gate, grad_up, grad_down


def solution(mesh):
    rows = P(("groups", "expert", "dp"), None)
    weights = P(("expert", "dp"), None)
    return jax.shard_map(
        local,
        mesh=mesh,
        in_specs=(rows,) * 4 + (weights,) * 3,
        out_specs=(rows,) * 5,
        check_vma=False,
    )
```

```python
import functools

import jax
import jax.numpy as jnp
from jax import lax
from jax.experimental import pallas as pl
from jax.experimental.pallas import tpu as pltpu
from jax.sharding import PartitionSpec as P

SPAN = 8
CAP = 6
ROWS = 16
LANE = 128
FIRST = (((0,), (0,)), ((), ()))
LAST = (((1,), (1,)), ((), ()))
F32 = jnp.float32
BF16 = jnp.bfloat16


def loop(count, body):
    if count <= 2:
        for i in range(count):
            body(i)
    else:
        pl.loop(0, count)(body)


def exchange_kernel(
    experts,
    tokens_ref, grad_ref, ids_ref, gates_ref, wg_ref, wu_ref, wd_ref,
    gt_ref, gg_ref, gwg_out, gwu_out, gwd_out,
    sel_ref, fin, grads_v, tok_v, dy_v, w_v, send, buf, tail, act, dxb, rc, r1,
    in_sem, out_sem, s1_s, s1_r, a1_s, a1_r, ac_s, ac_r,
    rc_s, rc_r, r1_s, r1_r, r0_s, r0_r,
):
    features = tok_v.shape[1]
    half = features // 2
    hid = wg_ref.shape[0]
    dp = lax.axis_index("dp")
    flat = lax.axis_index("expert") * 2 + dp
    octet = flat // SPAN
    pos = flat % SPAN
    bit1 = (pos // 2) % 2
    bit2 = pos // 4
    step_c = 1 - 2 * dp
    first = 2 - 4 * bit1
    second = 4 - 8 * bit2
    offsets = (0, first, second, first + second)

    def dev(index):
        return {"expert": index // 2, "dp": index % 2}

    barrier = pltpu.get_barrier_semaphore()
    for step in (first, second, first + second, step_c):
        pl.semaphore_signal(barrier, 1, device_id=dev(flat + step), device_id_type=pl.DeviceIdType.MESH)

    def greet(i):
        other = lax.rem(octet + i + 1, experts) * SPAN + pos
        pl.semaphore_signal(barrier, 1, device_id=dev(other), device_id_type=pl.DeviceIdType.MESH)

    loop(experts - 1, greet)

    loads = [
        pltpu.make_async_copy(tokens_ref, tok_v, in_sem.at[0]),
        pltpu.make_async_copy(grad_ref, dy_v, in_sem.at[1]),
        pltpu.make_async_copy(wg_ref, w_v.at[pl.ds(0, hid)], in_sem.at[2]),
        pltpu.make_async_copy(wu_ref, w_v.at[pl.ds(hid, hid)], in_sem.at[3]),
        pltpu.make_async_copy(wd_ref, w_v.at[pl.ds(2 * hid, hid)], in_sem.at[4]),
    ]
    for copy in loads:
        copy.start()

    count = ids_ref.shape[1]
    deep = experts * ROWS
    row = lax.broadcasted_iota(jnp.int32, (deep, count), 0)
    row_expert = row // ROWS
    row_slot = row % 8
    row_dy = (row // 8) % 2
    member = jnp.zeros((deep, count), F32)
    gate = jnp.zeros((deep, count), F32)
    for s in range(ids_ref.shape[0]):
        hit = ids_ref[s : s + 1, :] == row_expert
        member = member + jnp.where(hit, 1.0, 0.0)
        gate = gate + jnp.where(hit, gates_ref[s : s + 1, :], 0.0)
    upper = jnp.where(
        lax.broadcasted_iota(jnp.int32, (count, count), 0)
        <= lax.broadcasted_iota(jnp.int32, (count, count), 1),
        1.0, 0.0,
    ).astype(BF16)
    rank = jnp.dot(member.astype(BF16), upper, preferred_element_type=F32)

    def choose(wanted):
        chosen = jnp.where((member > 0.5) & (rank == wanted.astype(F32)), 1.0, 0.0)
        return (
            chosen,
            jnp.where(row_dy == 0, chosen, 0.0).astype(BF16),
            jnp.where(row_dy == 1, chosen, 0.0).astype(BF16),
        )

    chosen, sel_x, sel_dy = choose(jnp.where(row_slot < CAP, row_slot + 1, -1))
    weight = jnp.sum(chosen * gate, axis=1, keepdims=True)
    weight_hi = weight.astype(BF16).astype(F32)
    row_gate = jnp.where(row_dy == 0, weight_hi, weight - weight_hi)
    sel_ref[0] = sel_x
    sel_ref[1] = sel_dy
    tile = features // 4
    main = 3 * tile
    send[:, :, main:] = jnp.broadcast_to(row_gate[:, :1], (deep, LANE)).astype(BF16).reshape(experts, ROWS, LANE)
    loads[0].wait()
    loads[1].wait()
    for c in range(3):
        cols = pl.ds(c * tile, tile)
        _, end_x, end_dy = choose(jnp.where(row_slot < CAP, -1, (row_slot - CAP) * 3 + c + 1))
        block = (
            jnp.dot(sel_x, tok_v[:, cols], preferred_element_type=F32)
            + jnp.dot(sel_dy, dy_v[:, cols], preferred_element_type=F32)
            + jnp.dot(end_x, tok_v[:, main:], preferred_element_type=F32)
            + jnp.dot(end_dy, dy_v[:, main:], preferred_element_type=F32)
        )
        send[:, :, cols] = block.astype(BF16).reshape(experts, ROWS, tile)
    buf[flat] = send[octet]
    pl.semaphore_wait(barrier, 4 + experts - 1)

    def remote(src, dst, ssem, rsem, index):
        return pltpu.make_async_remote_copy(
            src_ref=src, dst_ref=dst, send_sem=ssem, recv_sem=rsem,
            device_id=dev(index), device_id_type=pl.DeviceIdType.MESH,
        )

    def source(d):
        return lax.rem(octet - d + experts, experts)

    def s1(i):
        other = lax.rem(octet + i + 1, experts)
        return remote(send.at[other], buf.at[flat], s1_s.at[i], s1_r.at[i], other * SPAN + pos)

    def pass_on(slot, ssem, rsem, index):
        return remote(buf.at[slot], buf.at[slot], ssem, rsem, index)

    def base(d):
        return source(d) * SPAN + pos

    def a1(d, k):
        return pass_on(base(d), a1_s.at[d, k - 1], a1_r.at[d, k - 1], flat + offsets[k])

    def ac(d, k):
        return pass_on(base(d) + offsets[k], ac_s.at[d, k], ac_r.at[d, k], flat + step_c)

    def own(d):
        for k in (3, 1, 2):
            a1(d, k).start()
        ac(d, 0).start()

    def to_core(d):
        for k in (1, 2, 3):
            a1(d, k).wait_recv()
            ac(d, k).start()

    loop(experts - 1, lambda i: s1(i).start())
    own(0)

    def after_s1(i):
        s1(i).wait_recv()
        own(i + 1)

    to_core(0)
    loop(experts - 1, after_s1)
    for copy in loads[2:]:
        copy.wait()

    deep_f = SPAN * ROWS
    to_row = lax.broadcasted_iota(jnp.int32, (deep_f, deep_f), 0)
    from_row = lax.broadcasted_iota(jnp.int32, (deep_f, deep_f), 1)
    to_slot = to_row % 8
    kept = (to_slot < CAP) & (from_row == (to_row // 8) * 8 + CAP + to_slot // 3)

    def compute(d):
        for k in range(4):
            ac(d, k).wait_recv()
        rows = pl.ds(source(d) * SPAN, SPAN)
        total = jnp.zeros((deep_f, 3 * hid), F32)
        ends = jnp.zeros((deep_f, tile), F32)
        for c in range(3):
            cols = pl.ds(c * tile, tile)
            piece = buf[rows, :, cols].reshape(deep_f, tile)
            total = total + lax.dot_general(piece, w_v[:, cols], LAST, preferred_element_type=F32)
            move = jnp.where(kept & (to_slot % 3 == c), 1.0, 0.0).astype(BF16)
            ends = ends + jnp.dot(move, piece, preferred_element_type=F32)
        ends = ends.astype(BF16)
        tail[rows] = ends.reshape(SPAN, ROWS, tile)
        total = total + lax.dot_general(ends, w_v[:, main:], LAST, preferred_element_type=F32)
        total = total.reshape(SPAN, 2, 8, 3 * hid)
        from_x = total[:, 0].reshape(SPAN * 8, 3 * hid)
        from_dy = total[:, 1].reshape(SPAN * 8, 3 * hid)
        pre_gate = from_x[:, :hid]
        pre_up = from_x[:, hid : 2 * hid]
        back = from_dy[:, 2 * hid :]
        packed = buf[rows, :, pl.ds(main, LANE)].astype(F32)
        weight = (packed[:, :8] + packed[:, 8:]).reshape(SPAN * 8, LANE)
        sig = jax.nn.sigmoid(pre_gate)
        silu = pre_gate * sig
        hidden = silu * pre_up
        dots = jnp.sum(hidden.astype(BF16).astype(F32) * back, axis=1, keepdims=True)
        grad_hidden = back * weight
        grad_gate = grad_hidden * pre_up * sig * (1.0 + pre_gate * (1.0 - sig))
        grad_up = grad_hidden * silu
        down = (hidden * weight).reshape(SPAN, 8, hid)
        none = jnp.zeros((SPAN, 8, hid), F32)
        upper = jnp.concatenate([grad_gate.reshape(SPAN, 8, hid), grad_up.reshape(SPAN, 8, hid), none], axis=2)
        under = jnp.concatenate([none, none, down], axis=2)
        act[rows] = jnp.concatenate([upper, under], axis=1).astype(BF16)
        pair = jnp.concatenate([grad_gate, grad_up], axis=1).astype(BF16)
        spread = jnp.broadcast_to(dots, (SPAN * 8, LANE)).reshape(SPAN, 8, LANE)
        dxb[rows, :, pl.ds(half, LANE)] = jnp.concatenate([spread, spread], axis=1).astype(BF16)
        step = half // 2
        for c in range(2):
            left = jnp.dot(pair, w_v[: 2 * hid, c * step : (c + 1) * step], preferred_element_type=F32)
            right = jnp.dot(
                pair, w_v[: 2 * hid, half + c * step : half + (c + 1) * step], preferred_element_type=F32
            )
            dxb[rows, :, pl.ds(c * step, step)] = jnp.concatenate(
                [left.reshape(SPAN, 8, step), right.reshape(SPAN, 8, step)], axis=1
            ).astype(BF16)


    def back_core(d, k):
        return remote(
            dxb.at[base(d) + step_c + offsets[k]], rc.at[d, k], rc_s.at[d, k], rc_r.at[d, k], flat + step_c
        )

    def back(d, k):
        return remote(
            dxb.at[base(d) + offsets[k]], r1.at[d, k - 1], r1_s.at[d, k - 1], r1_r.at[d, k - 1], flat + offsets[k]
        )

    def home(i):
        to = source(i + 1)
        return remote(dxb.at[base(i + 1)], fin.at[octet], r0_s.at[i], r0_r.at[i], to * SPAN + pos)

    def add(slot, piece):
        dxb[slot] = (dxb[slot].astype(F32) + piece.astype(F32)).astype(BF16)

    def start_core(d):
        for k in (3, 1, 2, 0):
            back_core(d, k).start()

    def sum_core(d):
        for k in (3, 1, 2, 0):
            back_core(d, k).wait_recv()
            add(base(d) + offsets[k], rc[d, k])
            if k > 0:
                back(d, k).start()

    def sum_back(d):
        for k in (1, 2, 3):
            back(d, k).wait_recv()
        pieces = dxb[base(d)].astype(F32)
        for k in range(3):
            pieces = pieces + r1[d, k].astype(F32)
        return pieces.astype(BF16)

    def weight_grads(c):
        rows = buf[:, :, c * tile : (c + 1) * tile] if c < 3 else tail[...]
        grads = lax.dot_general(
            act[...].reshape(experts * deep_f, 3 * hid), rows.reshape(experts * deep_f, tile), FIRST,
            preferred_element_type=F32,
        )
        grads_v[:, pl.ds(c * tile, tile)] = grads.astype(BF16)

    compute(0)
    start_core(0)
    loop(experts - 1, lambda i: to_core(i + 1))
    sum_core(0)

    def far_compute(i):
        compute(i + 1)
        start_core(i + 1)

    loop(experts - 1, far_compute)
    loop(experts - 1, lambda i: sum_core(i + 1))
    weight_grads(0)
    weight_grads(1)

    def far_home(i):
        dxb[base(i + 1)] = sum_back(i + 1)
        home(i).start()

    loop(experts - 1, far_home)
    weight_grads(2)
    weight_grads(3)
    stores = [
        pltpu.make_async_copy(grads_v.at[pl.ds(i * hid, hid)], out, out_sem.at[i])
        for i, out in enumerate((gwg_out, gwu_out, gwd_out))
    ]
    for copy in stores:
        copy.start()
    fin[octet] = sum_back(0)
    loop(experts - 1, lambda i: home(i).wait_recv())

    gathered = fin[...].reshape(deep, half + LANE)
    step = half // 2
    for h in range(2):
        for c in range(2):
            gt_ref[:, h * half + c * step : h * half + (c + 1) * step] = lax.dot_general(
                sel_ref[h], gathered[:, c * step : (c + 1) * step], FIRST, preferred_element_type=F32
            ).astype(BF16)
    dots = lax.dot_general(gathered[:, half:], sel_ref[0], FIRST, preferred_element_type=F32)
    gg_ref[...] = jnp.where(ids_ref[...] < experts, dots[: ids_ref.shape[0]], 0.0)

    def finish(d):
        for k in range(4):
            ac(d, k).wait_send()
            back_core(d, k).wait_send()
        for k in (1, 2, 3):
            a1(d, k).wait_send()
            back(d, k).wait_send()

    loop(experts, finish)

    def finish_far(i):
        s1(i).wait_send()
        home(i).wait_send()

    loop(experts - 1, finish_far)
    for copy in stores:
        copy.wait()


def local(tokens, grad_out, expert_ids, gate_weights, w_gate, w_up, w_down):
    flat_count = lax.axis_size(("expert", "dp"))
    experts = flat_count // SPAN
    count, features = tokens.shape
    hid = w_gate.shape[0]
    half = features // 2
    tiles = 4
    tile = features // tiles
    wide = 3 * tile + LANE
    deep = experts * ROWS
    ids_t, gates_t = expert_ids.T, gate_weights.T
    narrow = half + LANE
    slots = experts * SPAN
    far = max(experts - 1, 1)
    vmem = pl.BlockSpec(memory_space=pltpu.VMEM)
    anyspace = pl.BlockSpec(memory_space=pl.ANY)
    sem = pltpu.SemaphoreType.DMA
    full = jax.ShapeDtypeStruct((hid, features), BF16)
    grad_tokens, grad_gates, grad_gate, grad_up, grad_down = pl.pallas_call(
        functools.partial(exchange_kernel, experts),
        out_shape=(
            jax.ShapeDtypeStruct((count, features), BF16),
            jax.ShapeDtypeStruct(gates_t.shape, F32),
            full, full, full,
        ),
        in_specs=[anyspace, anyspace, vmem, vmem, anyspace, anyspace, anyspace],
        out_specs=(vmem, vmem, anyspace, anyspace, anyspace),
        scratch_shapes=[
            pltpu.VMEM((2, deep, count), BF16),
            pltpu.VMEM((experts, ROWS, narrow), BF16),
            pltpu.VMEM((3 * hid, features), BF16),
            pltpu.VMEM((count, features), BF16),
            pltpu.VMEM((count, features), BF16),
            pltpu.VMEM((3 * hid, features), BF16),
            pltpu.VMEM((experts, ROWS, wide), BF16),
            pltpu.VMEM((slots, ROWS, wide), BF16),
            pltpu.VMEM((slots, ROWS, tile), BF16),
            pltpu.VMEM((slots, ROWS, 3 * hid), BF16),
            pltpu.VMEM((slots, ROWS, narrow), BF16),
            pltpu.VMEM((experts, 4, ROWS, narrow), BF16),
            pltpu.VMEM((experts, 3, ROWS, narrow), BF16),
            sem((7,)), sem((3,)),
            sem((far,)), sem((far,)),
            sem((experts, 3)), sem((experts, 3)),
            sem((experts, 4)), sem((experts, 4)),
            sem((experts, 4)), sem((experts, 4)),
            sem((experts, 3)), sem((experts, 3)),
            sem((far,)), sem((far,)),
        ],
        compiler_params=pltpu.CompilerParams(
            collective_id=0, has_side_effects=True, vmem_limit_bytes=60 * 1024 * 1024
        ),
    )(tokens, grad_out, ids_t, gates_t, w_gate, w_up, w_down)
    return grad_tokens, grad_gates.T, grad_gate, grad_up, grad_down


def solution(mesh):
    rows = P(("groups", "expert", "dp"), None)
    weights = P(("expert", "dp"), None)
    return jax.shard_map(
        local,
        mesh=mesh,
        in_specs=(rows,) * 4 + (weights,) * 3,
        out_specs=(rows,) * 5,
        check_vma=False,
    )
```

```python
import functools

import jax
import jax.numpy as jnp
from jax import lax
from jax.experimental import pallas as pl
from jax.experimental.pallas import tpu as pltpu
from jax.sharding import PartitionSpec as P

SPAN = 8
CAP = 6
ROWS = 16
LANE = 128
FIRST = (((0,), (0,)), ((), ()))
LAST = (((1,), (1,)), ((), ()))
F32 = jnp.float32
BF16 = jnp.bfloat16


def loop(count, body):
    if count <= 2:
        for i in range(count):
            body(i)
    else:
        pl.loop(0, count)(body)


def exchange_kernel(
    experts,
    tokens_ref, grad_ref, ids_ref, gates_ref, wg_ref, wu_ref, wd_ref,
    gt_ref, gg_ref, gwg_out, gwu_out, gwd_out,
    sel_ref, fin, grads_v, tok_v, dy_v, w_v, send, buf, tail, act, dxb, rc, r1,
    in_sem, out_sem, s1_s, s1_r, a1_s, a1_r, ac_s, ac_r,
    rc_s, rc_r, r1_s, r1_r, r0_s, r0_r,
):
    features = tok_v.shape[1]
    half = features // 2
    hid = wg_ref.shape[0]
    dp = lax.axis_index("dp")
    flat = lax.axis_index("expert") * 2 + dp
    octet = flat // SPAN
    pos = flat % SPAN
    bit1 = (pos // 2) % 2
    bit2 = pos // 4
    step_c = 1 - 2 * dp
    first = 2 - 4 * bit1
    second = 4 - 8 * bit2
    offsets = (0, first, second, first + second)

    def dev(index):
        return {"expert": index // 2, "dp": index % 2}

    barrier = pltpu.get_barrier_semaphore()
    for step in (first, second, first + second, step_c):
        pl.semaphore_signal(barrier, 1, device_id=dev(flat + step), device_id_type=pl.DeviceIdType.MESH)

    def greet(i):
        other = lax.rem(octet + i + 1, experts) * SPAN + pos
        pl.semaphore_signal(barrier, 1, device_id=dev(other), device_id_type=pl.DeviceIdType.MESH)

    loop(experts - 1, greet)

    loads = [
        pltpu.make_async_copy(tokens_ref, tok_v, in_sem.at[0]),
        pltpu.make_async_copy(grad_ref, dy_v, in_sem.at[1]),
        pltpu.make_async_copy(wg_ref, w_v.at[pl.ds(0, hid)], in_sem.at[2]),
        pltpu.make_async_copy(wu_ref, w_v.at[pl.ds(hid, hid)], in_sem.at[3]),
        pltpu.make_async_copy(wd_ref, w_v.at[pl.ds(2 * hid, hid)], in_sem.at[4]),
    ]
    for copy in loads:
        copy.start()

    count = ids_ref.shape[1]
    deep = experts * ROWS
    row = lax.broadcasted_iota(jnp.int32, (deep, count), 0)
    row_expert = row // ROWS
    row_slot = row % 8
    row_dy = (row // 8) % 2
    member = jnp.zeros((deep, count), F32)
    gate = jnp.zeros((deep, count), F32)
    for s in range(ids_ref.shape[0]):
        hit = ids_ref[s : s + 1, :] == row_expert
        member = member + jnp.where(hit, 1.0, 0.0)
        gate = gate + jnp.where(hit, gates_ref[s : s + 1, :], 0.0)
    upper = jnp.where(
        lax.broadcasted_iota(jnp.int32, (count, count), 0)
        <= lax.broadcasted_iota(jnp.int32, (count, count), 1),
        1.0, 0.0,
    ).astype(BF16)
    rank = jnp.dot(member.astype(BF16), upper, preferred_element_type=F32)

    def choose(wanted):
        chosen = jnp.where((member > 0.5) & (rank == wanted.astype(F32)), 1.0, 0.0)
        return (
            chosen,
            jnp.where(row_dy == 0, chosen, 0.0).astype(BF16),
            jnp.where(row_dy == 1, chosen, 0.0).astype(BF16),
        )

    chosen, sel_x, sel_dy = choose(jnp.where(row_slot < CAP, row_slot + 1, -1))
    weight = jnp.sum(chosen * gate, axis=1, keepdims=True)
    weight_hi = weight.astype(BF16).astype(F32)
    row_gate = jnp.where(row_dy == 0, weight_hi, weight - weight_hi)
    sel_ref[0] = sel_x
    sel_ref[1] = sel_dy
    tile = features // 4
    main = 3 * tile
    send[:, :, main:] = jnp.broadcast_to(row_gate[:, :1], (deep, LANE)).astype(BF16).reshape(experts, ROWS, LANE)
    loads[0].wait()
    loads[1].wait()
    for c in range(3):
        cols = pl.ds(c * tile, tile)
        _, end_x, end_dy = choose(jnp.where(row_slot < CAP, -1, (row_slot - CAP) * 3 + c + 1))
        block = (
            jnp.dot(sel_x, tok_v[:, cols], preferred_element_type=F32)
            + jnp.dot(sel_dy, dy_v[:, cols], preferred_element_type=F32)
            + jnp.dot(end_x, tok_v[:, main:], preferred_element_type=F32)
            + jnp.dot(end_dy, dy_v[:, main:], preferred_element_type=F32)
        )
        send[:, :, cols] = block.astype(BF16).reshape(experts, ROWS, tile)
    buf[flat] = send[octet]
    pl.semaphore_wait(barrier, 4 + experts - 1)

    def remote(src, dst, ssem, rsem, index):
        return pltpu.make_async_remote_copy(
            src_ref=src, dst_ref=dst, send_sem=ssem, recv_sem=rsem,
            device_id=dev(index), device_id_type=pl.DeviceIdType.MESH,
        )

    def source(d):
        return lax.rem(octet - d + experts, experts)

    def s1(i):
        other = lax.rem(octet + i + 1, experts)
        return remote(send.at[other], buf.at[flat], s1_s.at[i], s1_r.at[i], other * SPAN + pos)

    def pass_on(slot, ssem, rsem, index):
        return remote(buf.at[slot], buf.at[slot], ssem, rsem, index)

    def base(d):
        return source(d) * SPAN + pos

    def a1(d, k):
        return pass_on(base(d), a1_s.at[d, k - 1], a1_r.at[d, k - 1], flat + offsets[k])

    def ac(d, k):
        return pass_on(base(d) + offsets[k], ac_s.at[d, k], ac_r.at[d, k], flat + step_c)

    def own(d):
        for k in (3, 1, 2):
            a1(d, k).start()
        ac(d, 0).start()

    def to_core(d):
        for k in (1, 2, 3):
            a1(d, k).wait_recv()
            ac(d, k).start()

    loop(experts - 1, lambda i: s1(i).start())
    own(0)

    def after_s1(i):
        s1(i).wait_recv()
        own(i + 1)

    to_core(0)
    loop(experts - 1, after_s1)
    for copy in loads[2:]:
        copy.wait()

    deep_f = SPAN * ROWS
    to_row = lax.broadcasted_iota(jnp.int32, (deep_f, deep_f), 0)
    from_row = lax.broadcasted_iota(jnp.int32, (deep_f, deep_f), 1)
    to_slot = to_row % 8
    kept = (to_slot < CAP) & (from_row == (to_row // 8) * 8 + CAP + to_slot // 3)

    def compute(d):
        for k in range(4):
            ac(d, k).wait_recv()
        rows = pl.ds(source(d) * SPAN, SPAN)
        total = jnp.zeros((deep_f, 3 * hid), F32)
        ends = jnp.zeros((deep_f, tile), F32)
        for c in range(3):
            cols = pl.ds(c * tile, tile)
            piece = buf[rows, :, cols].reshape(deep_f, tile)
            total = total + lax.dot_general(piece, w_v[:, cols], LAST, preferred_element_type=F32)
            move = jnp.where(kept & (to_slot % 3 == c), 1.0, 0.0).astype(BF16)
            ends = ends + jnp.dot(move, piece, preferred_element_type=F32)
        ends = ends.astype(BF16)
        tail[rows] = ends.reshape(SPAN, ROWS, tile)
        total = total + lax.dot_general(ends, w_v[:, main:], LAST, preferred_element_type=F32)
        total = total.reshape(SPAN, 2, 8, 3 * hid)
        from_x = total[:, 0].reshape(SPAN * 8, 3 * hid)
        from_dy = total[:, 1].reshape(SPAN * 8, 3 * hid)
        pre_gate = from_x[:, :hid]
        pre_up = from_x[:, hid : 2 * hid]
        back = from_dy[:, 2 * hid :]
        packed = buf[rows, :, pl.ds(main, LANE)].astype(F32)
        weight = (packed[:, :8] + packed[:, 8:]).reshape(SPAN * 8, LANE)
        sig = jax.nn.sigmoid(pre_gate)
        silu = pre_gate * sig
        hidden = silu * pre_up
        dots = jnp.sum(hidden.astype(BF16).astype(F32) * back, axis=1, keepdims=True)
        grad_hidden = back * weight
        grad_gate = grad_hidden * pre_up * sig * (1.0 + pre_gate * (1.0 - sig))
        grad_up = grad_hidden * silu
        down = (hidden * weight).reshape(SPAN, 8, hid)
        none = jnp.zeros((SPAN, 8, hid), F32)
        upper = jnp.concatenate([grad_gate.reshape(SPAN, 8, hid), grad_up.reshape(SPAN, 8, hid), none], axis=2)
        under = jnp.concatenate([none, none, down], axis=2)
        act[rows] = jnp.concatenate([upper, under], axis=1).astype(BF16)
        pair = jnp.concatenate([grad_gate, grad_up], axis=1).astype(BF16)
        spread = jnp.broadcast_to(dots, (SPAN * 8, LANE)).reshape(SPAN, 8, LANE)
        dxb[rows, :, pl.ds(half, LANE)] = jnp.concatenate([spread, spread], axis=1).astype(BF16)
        step = half // 2
        for c in range(2):
            left = jnp.dot(pair, w_v[: 2 * hid, c * step : (c + 1) * step], preferred_element_type=F32)
            right = jnp.dot(
                pair, w_v[: 2 * hid, half + c * step : half + (c + 1) * step], preferred_element_type=F32
            )
            dxb[rows, :, pl.ds(c * step, step)] = jnp.concatenate(
                [left.reshape(SPAN, 8, step), right.reshape(SPAN, 8, step)], axis=1
            ).astype(BF16)


    def back_core(d, k):
        return remote(
            dxb.at[base(d) + step_c + offsets[k]], rc.at[d, k], rc_s.at[d, k], rc_r.at[d, k], flat + step_c
        )

    def back(d, k):
        return remote(
            dxb.at[base(d) + offsets[k]], r1.at[d, k - 1], r1_s.at[d, k - 1], r1_r.at[d, k - 1], flat + offsets[k]
        )

    def home(i):
        to = source(i + 1)
        return remote(dxb.at[base(i + 1)], fin.at[octet], r0_s.at[i], r0_r.at[i], to * SPAN + pos)

    def add(slot, piece):
        dxb[slot] = (dxb[slot].astype(F32) + piece.astype(F32)).astype(BF16)

    def start_core(d):
        for k in (3, 1, 2, 0):
            back_core(d, k).start()

    def sum_core(d):
        for k in (3, 1, 2, 0):
            back_core(d, k).wait_recv()
            add(base(d) + offsets[k], rc[d, k])
            if k > 0:
                back(d, k).start()

    def sum_back(d):
        for k in (1, 2, 3):
            back(d, k).wait_recv()
        pieces = dxb[base(d)].astype(F32)
        for k in range(3):
            pieces = pieces + r1[d, k].astype(F32)
        return pieces.astype(BF16)

    def weight_grads(c):
        rows = buf[:, :, c * tile : (c + 1) * tile] if c < 3 else tail[...]
        grads = lax.dot_general(
            act[...].reshape(experts * deep_f, 3 * hid), rows.reshape(experts * deep_f, tile), FIRST,
            preferred_element_type=F32,
        )
        grads_v[:, pl.ds(c * tile, tile)] = grads.astype(BF16)

    compute(0)
    start_core(0)
    loop(experts - 1, lambda i: to_core(i + 1))
    sum_core(0)

    def far_compute(i):
        compute(i + 1)
        start_core(i + 1)

    loop(experts - 1, far_compute)
    loop(experts - 1, lambda i: sum_core(i + 1))
    weight_grads(0)
    weight_grads(1)

    def far_home(i):
        dxb[base(i + 1)] = sum_back(i + 1)
        home(i).start()

    loop(experts - 1, far_home)
    weight_grads(2)
    weight_grads(3)
    stores = [
        pltpu.make_async_copy(grads_v.at[pl.ds(i * hid, hid)], out, out_sem.at[i])
        for i, out in enumerate((gwg_out, gwu_out, gwd_out))
    ]
    for copy in stores:
        copy.start()
    fin[octet] = sum_back(0)
    loop(experts - 1, lambda i: home(i).wait_recv())

    gathered = fin[...].reshape(deep, half + LANE)
    step = half // 2
    for h in range(2):
        for c in range(2):
            gt_ref[:, h * half + c * step : h * half + (c + 1) * step] = lax.dot_general(
                sel_ref[h], gathered[:, c * step : (c + 1) * step], FIRST, preferred_element_type=F32
            ).astype(BF16)
    dots = lax.dot_general(gathered[:, half:], sel_ref[0], FIRST, preferred_element_type=F32)
    gg_ref[...] = jnp.where(ids_ref[...] < experts, dots[: ids_ref.shape[0]], 0.0)

    def finish(d):
        for k in range(4):
            ac(d, k).wait_send()
            back_core(d, k).wait_send()
        for k in (1, 2, 3):
            a1(d, k).wait_send()
            back(d, k).wait_send()

    loop(experts, finish)

    def finish_far(i):
        s1(i).wait_send()
        home(i).wait_send()

    loop(experts - 1, finish_far)
    for copy in stores:
        copy.wait()


def hand_over_kernel(cuts, *refs):
    count = len(cuts)
    sources, results, held = refs[:count], refs[count : 2 * count], refs[2 * count : 3 * count]
    in_sem, out_sem = refs[3 * count :]
    arrive, leave = [], []
    for i in range(count):
        size = sources[i].shape[0] // cuts[i]
        for c in range(cuts[i]):
            rows = pl.ds(c * size, size)
            n = len(arrive)
            arrive.append(pltpu.make_async_copy(sources[i].at[rows], held[i].at[rows], in_sem.at[n]))
            leave.append(pltpu.make_async_copy(held[i].at[rows], results[i].at[rows], out_sem.at[n]))
    for copy in arrive:
        copy.start()
    for copy, after in zip(arrive, leave):
        copy.wait()
        after.start()
    for copy in leave:
        copy.wait()


def local(tokens, grad_out, expert_ids, gate_weights, w_gate, w_up, w_down):
    flat_count = lax.axis_size(("expert", "dp"))
    experts = flat_count // SPAN
    count, features = tokens.shape
    hid = w_gate.shape[0]
    half = features // 2
    tiles = 4
    tile = features // tiles
    wide = 3 * tile + LANE
    deep = experts * ROWS
    ids_t, gates_t = expert_ids.T, gate_weights.T
    narrow = half + LANE
    slots = experts * SPAN
    far = max(experts - 1, 1)
    vmem = pl.BlockSpec(memory_space=pltpu.VMEM)
    anyspace = pl.BlockSpec(memory_space=pl.ANY)
    sem = pltpu.SemaphoreType.DMA
    full = jax.ShapeDtypeStruct((hid, features), BF16)
    made = pl.pallas_call(
        functools.partial(exchange_kernel, experts),
        out_shape=(
            jax.ShapeDtypeStruct((count, features), BF16),
            jax.ShapeDtypeStruct(gates_t.shape, F32),
            full, full, full,
        ),
        in_specs=[anyspace, anyspace, vmem, vmem, anyspace, anyspace, anyspace],
        out_specs=(vmem, vmem, anyspace, anyspace, anyspace),
        scratch_shapes=[
            pltpu.VMEM((2, deep, count), BF16),
            pltpu.VMEM((experts, ROWS, narrow), BF16),
            pltpu.VMEM((3 * hid, features), BF16),
            pltpu.VMEM((count, features), BF16),
            pltpu.VMEM((count, features), BF16),
            pltpu.VMEM((3 * hid, features), BF16),
            pltpu.VMEM((experts, ROWS, wide), BF16),
            pltpu.VMEM((slots, ROWS, wide), BF16),
            pltpu.VMEM((slots, ROWS, tile), BF16),
            pltpu.VMEM((slots, ROWS, 3 * hid), BF16),
            pltpu.VMEM((slots, ROWS, narrow), BF16),
            pltpu.VMEM((experts, 4, ROWS, narrow), BF16),
            pltpu.VMEM((experts, 3, ROWS, narrow), BF16),
            sem((7,)), sem((3,)),
            sem((far,)), sem((far,)),
            sem((experts, 3)), sem((experts, 3)),
            sem((experts, 4)), sem((experts, 4)),
            sem((experts, 4)), sem((experts, 4)),
            sem((experts, 3)), sem((experts, 3)),
            sem((far,)), sem((far,)),
        ],
        compiler_params=pltpu.CompilerParams(
            collective_id=0, has_side_effects=True, vmem_limit_bytes=60 * 1024 * 1024
        ),
    )(tokens, grad_out, ids_t, gates_t, w_gate, w_up, w_down)
    cuts = (2, 1, 2, 2, 2)
    grad_tokens, grad_gates, grad_gate, grad_up, grad_down = pl.pallas_call(
        functools.partial(hand_over_kernel, cuts),
        out_shape=tuple(jax.ShapeDtypeStruct(a.shape, a.dtype) for a in made),
        in_specs=[anyspace] * len(cuts),
        out_specs=(anyspace,) * len(cuts),
        scratch_shapes=[pltpu.VMEM(a.shape, a.dtype) for a in made] + [sem((sum(cuts),)), sem((sum(cuts),))],
        compiler_params=pltpu.CompilerParams(vmem_limit_bytes=60 * 1024 * 1024),
    )(*made)
    return grad_tokens, grad_gates.T, grad_gate, grad_up, grad_down


def solution(mesh):
    rows = P(("groups", "expert", "dp"), None)
    weights = P(("expert", "dp"), None)
    return jax.shard_map(
        local,
        mesh=mesh,
        in_specs=(rows,) * 4 + (weights,) * 3,
        out_specs=(rows,) * 5,
        check_vma=False,
    )
```

```python
import functools

import jax
import jax.numpy as jnp
from jax import lax
from jax.experimental import pallas as pl
from jax.experimental.pallas import tpu as pltpu
from jax.sharding import PartitionSpec as P

SPAN = 8
CAP = 6
ROWS = 16
LANE = 128
FIRST = (((0,), (0,)), ((), ()))
LAST = (((1,), (1,)), ((), ()))
F32 = jnp.float32
BF16 = jnp.bfloat16


def loop(count, body):
    if count <= 2:
        for i in range(count):
            body(i)
    else:
        pl.loop(0, count)(body)


def exchange_kernel(
    experts,
    tokens_ref, grad_ref, ids_ref, gates_ref, wg_ref, wu_ref, wd_ref,
    gt_ref, gg_ref, gwg_out, gwu_out, gwd_out,
    sel_ref, fin, grads_v, tok_v, dy_v, w_v, send, buf, tail, act, dxb, rc, r1,
    in_sem, out_sem, s1_s, s1_r, a1_s, a1_r, ac_s, ac_r,
    rc_s, rc_r, r1_s, r1_r, r0_s, r0_r,
):
    features = tok_v.shape[1]
    half = features // 2
    hid = wg_ref.shape[0]
    dp = lax.axis_index("dp")
    flat = lax.axis_index("expert") * 2 + dp
    octet = flat // SPAN
    pos = flat % SPAN
    bit1 = (pos // 2) % 2
    bit2 = pos // 4
    step_c = 1 - 2 * dp
    first = 2 - 4 * bit1
    second = 4 - 8 * bit2
    offsets = (0, first, second, first + second)

    def dev(index):
        return {"expert": index // 2, "dp": index % 2}

    barrier = pltpu.get_barrier_semaphore()
    for step in (first, second, first + second, step_c):
        pl.semaphore_signal(barrier, 1, device_id=dev(flat + step), device_id_type=pl.DeviceIdType.MESH)

    def greet(i):
        other = lax.rem(octet + i + 1, experts) * SPAN + pos
        pl.semaphore_signal(barrier, 1, device_id=dev(other), device_id_type=pl.DeviceIdType.MESH)

    loop(experts - 1, greet)

    loads = [
        pltpu.make_async_copy(tokens_ref, tok_v, in_sem.at[0]),
        pltpu.make_async_copy(grad_ref, dy_v, in_sem.at[1]),
        pltpu.make_async_copy(wg_ref, w_v.at[pl.ds(0, hid)], in_sem.at[2]),
        pltpu.make_async_copy(wu_ref, w_v.at[pl.ds(hid, hid)], in_sem.at[3]),
        pltpu.make_async_copy(wd_ref, w_v.at[pl.ds(2 * hid, hid)], in_sem.at[4]),
    ]
    for copy in loads:
        copy.start()

    count = ids_ref.shape[1]
    deep = experts * ROWS
    row = lax.broadcasted_iota(jnp.int32, (deep, count), 0)
    row_expert = row // ROWS
    row_slot = row % 8
    row_dy = (row // 8) % 2
    member = jnp.zeros((deep, count), F32)
    gate = jnp.zeros((deep, count), F32)
    for s in range(ids_ref.shape[0]):
        hit = ids_ref[s : s + 1, :] == row_expert
        member = member + jnp.where(hit, 1.0, 0.0)
        gate = gate + jnp.where(hit, gates_ref[s : s + 1, :], 0.0)
    upper = jnp.where(
        lax.broadcasted_iota(jnp.int32, (count, count), 0)
        <= lax.broadcasted_iota(jnp.int32, (count, count), 1),
        1.0, 0.0,
    ).astype(BF16)
    rank = jnp.dot(member.astype(BF16), upper, preferred_element_type=F32)

    def choose(wanted):
        chosen = jnp.where((member > 0.5) & (rank == wanted.astype(F32)), 1.0, 0.0)
        return (
            chosen,
            jnp.where(row_dy == 0, chosen, 0.0).astype(BF16),
            jnp.where(row_dy == 1, chosen, 0.0).astype(BF16),
        )

    chosen, sel_x, sel_dy = choose(jnp.where(row_slot < CAP, row_slot + 1, -1))
    weight = jnp.sum(chosen * gate, axis=1, keepdims=True)
    weight_hi = weight.astype(BF16).astype(F32)
    row_gate = jnp.where(row_dy == 0, weight_hi, weight - weight_hi)
    sel_ref[0] = sel_x
    sel_ref[1] = sel_dy
    tile = features // 4
    main = 3 * tile
    send[:, :, main:] = jnp.broadcast_to(row_gate[:, :1], (deep, LANE)).astype(BF16).reshape(experts, ROWS, LANE)
    loads[0].wait()
    loads[1].wait()
    for c in range(3):
        cols = pl.ds(c * tile, tile)
        _, end_x, end_dy = choose(jnp.where(row_slot < CAP, -1, (row_slot - CAP) * 3 + c + 1))
        block = (
            jnp.dot(sel_x, tok_v[:, cols], preferred_element_type=F32)
            + jnp.dot(sel_dy, dy_v[:, cols], preferred_element_type=F32)
            + jnp.dot(end_x, tok_v[:, main:], preferred_element_type=F32)
            + jnp.dot(end_dy, dy_v[:, main:], preferred_element_type=F32)
        )
        send[:, :, cols] = block.astype(BF16).reshape(experts, ROWS, tile)
    buf[flat] = send[octet]
    pl.semaphore_wait(barrier, 4 + experts - 1)

    def remote(src, dst, ssem, rsem, index):
        return pltpu.make_async_remote_copy(
            src_ref=src, dst_ref=dst, send_sem=ssem, recv_sem=rsem,
            device_id=dev(index), device_id_type=pl.DeviceIdType.MESH,
        )

    def source(d):
        return lax.rem(octet - d + experts, experts)

    part = (main + LANE) // 2
    parts = (pl.ds(0, part), pl.ds(part, part))

    def s1(i, p):
        other = lax.rem(octet + i + 1, experts)
        return remote(
            send.at[other, :, parts[p]], buf.at[flat, :, parts[p]], s1_s.at[i, p], s1_r.at[i, p], other * SPAN + pos
        )

    def pass_on(slot, p, ssem, rsem, index):
        return remote(buf.at[slot, :, parts[p]], buf.at[slot, :, parts[p]], ssem, rsem, index)

    def base(d):
        return source(d) * SPAN + pos

    def a1(d, k, p):
        return pass_on(base(d), p, a1_s.at[d, k - 1, p], a1_r.at[d, k - 1, p], flat + offsets[k])

    def ac(d, k, p):
        return pass_on(base(d) + offsets[k], p, ac_s.at[d, k, p], ac_r.at[d, k, p], flat + step_c)

    def own(d, p):
        for k in (3, 1, 2):
            a1(d, k, p).start()
        ac(d, 0, p).start()

    def to_core(d):
        for p in range(2):
            for k in (1, 2, 3):
                a1(d, k, p).wait_recv()
                ac(d, k, p).start()

    for p in range(2):
        loop(experts - 1, lambda i: s1(i, p).start())
    own(0, 0)
    own(0, 1)

    def after_s1(i):
        for p in range(2):
            s1(i, p).wait_recv()
            own(i + 1, p)

    loop(experts - 1, after_s1)
    to_core(0)
    for copy in loads[2:]:
        copy.wait()

    deep_f = SPAN * ROWS
    to_row = lax.broadcasted_iota(jnp.int32, (deep_f, deep_f), 0)
    from_row = lax.broadcasted_iota(jnp.int32, (deep_f, deep_f), 1)
    to_slot = to_row % 8
    kept = (to_slot < CAP) & (from_row == (to_row // 8) * 8 + CAP + to_slot // 3)

    def compute(d):
        for k in range(4):
            for p in range(2):
                ac(d, k, p).wait_recv()
        rows = pl.ds(source(d) * SPAN, SPAN)
        total = jnp.zeros((deep_f, 3 * hid), F32)
        ends = jnp.zeros((deep_f, tile), F32)
        for c in range(3):
            cols = pl.ds(c * tile, tile)
            piece = buf[rows, :, cols].reshape(deep_f, tile)
            total = total + lax.dot_general(piece, w_v[:, cols], LAST, preferred_element_type=F32)
            move = jnp.where(kept & (to_slot % 3 == c), 1.0, 0.0).astype(BF16)
            ends = ends + jnp.dot(move, piece, preferred_element_type=F32)
        ends = ends.astype(BF16)
        tail[rows] = ends.reshape(SPAN, ROWS, tile)
        total = total + lax.dot_general(ends, w_v[:, main:], LAST, preferred_element_type=F32)
        total = total.reshape(SPAN, 2, 8, 3 * hid)
        from_x = total[:, 0].reshape(SPAN * 8, 3 * hid)
        from_dy = total[:, 1].reshape(SPAN * 8, 3 * hid)
        pre_gate = from_x[:, :hid]
        pre_up = from_x[:, hid : 2 * hid]
        back = from_dy[:, 2 * hid :]
        packed = buf[rows, :, pl.ds(main, LANE)].astype(F32)
        weight = (packed[:, :8] + packed[:, 8:]).reshape(SPAN * 8, LANE)
        sig = jax.nn.sigmoid(pre_gate)
        silu = pre_gate * sig
        hidden = silu * pre_up
        dots = jnp.sum(hidden.astype(BF16).astype(F32) * back, axis=1, keepdims=True)
        grad_hidden = back * weight
        grad_gate = grad_hidden * pre_up * sig * (1.0 + pre_gate * (1.0 - sig))
        grad_up = grad_hidden * silu
        down = (hidden * weight).reshape(SPAN, 8, hid)
        none = jnp.zeros((SPAN, 8, hid), F32)
        upper = jnp.concatenate([grad_gate.reshape(SPAN, 8, hid), grad_up.reshape(SPAN, 8, hid), none], axis=2)
        under = jnp.concatenate([none, none, down], axis=2)
        act[rows] = jnp.concatenate([upper, under], axis=1).astype(BF16)
        pair = jnp.concatenate([grad_gate, grad_up], axis=1).astype(BF16)
        spread = jnp.broadcast_to(dots, (SPAN * 8, LANE)).reshape(SPAN, 8, LANE)
        dxb[rows, :, pl.ds(half, LANE)] = jnp.concatenate([spread, spread], axis=1).astype(BF16)
        step = half // 2
        for c in range(2):
            left = jnp.dot(pair, w_v[: 2 * hid, c * step : (c + 1) * step], preferred_element_type=F32)
            right = jnp.dot(
                pair, w_v[: 2 * hid, half + c * step : half + (c + 1) * step], preferred_element_type=F32
            )
            dxb[rows, :, pl.ds(c * step, step)] = jnp.concatenate(
                [left.reshape(SPAN, 8, step), right.reshape(SPAN, 8, step)], axis=1
            ).astype(BF16)


    def back_core(d, k):
        return remote(
            dxb.at[base(d) + step_c + offsets[k]], rc.at[d, k], rc_s.at[d, k], rc_r.at[d, k], flat + step_c
        )

    def back(d, k):
        return remote(
            dxb.at[base(d) + offsets[k]], r1.at[d, k - 1], r1_s.at[d, k - 1], r1_r.at[d, k - 1], flat + offsets[k]
        )

    def home(i):
        to = source(i + 1)
        return remote(dxb.at[base(i + 1)], fin.at[octet], r0_s.at[i], r0_r.at[i], to * SPAN + pos)

    def add(slot, piece):
        dxb[slot] = (dxb[slot].astype(F32) + piece.astype(F32)).astype(BF16)

    def start_core(d):
        for k in (3, 1, 2, 0):
            back_core(d, k).start()

    def sum_core(d):
        for k in (3, 1, 2, 0):
            back_core(d, k).wait_recv()
            add(base(d) + offsets[k], rc[d, k])
            if k > 0:
                back(d, k).start()

    def sum_back(d):
        for k in (1, 2, 3):
            back(d, k).wait_recv()
        pieces = dxb[base(d)].astype(F32)
        for k in range(3):
            pieces = pieces + r1[d, k].astype(F32)
        return pieces.astype(BF16)

    def weight_grads(c):
        rows = buf[:, :, c * tile : (c + 1) * tile] if c < 3 else tail[...]
        grads = lax.dot_general(
            act[...].reshape(experts * deep_f, 3 * hid), rows.reshape(experts * deep_f, tile), FIRST,
            preferred_element_type=F32,
        )
        grads_v[:, pl.ds(c * tile, tile)] = grads.astype(BF16)

    compute(0)
    start_core(0)
    loop(experts - 1, lambda i: to_core(i + 1))
    sum_core(0)

    def far_compute(i):
        compute(i + 1)
        start_core(i + 1)

    loop(experts - 1, far_compute)
    loop(experts - 1, lambda i: sum_core(i + 1))
    weight_grads(0)
    weight_grads(1)

    def far_home(i):
        dxb[base(i + 1)] = sum_back(i + 1)
        home(i).start()

    loop(experts - 1, far_home)
    weight_grads(2)
    weight_grads(3)
    stores = [
        pltpu.make_async_copy(grads_v.at[pl.ds(i * hid, hid)], out, out_sem.at[i])
        for i, out in enumerate((gwg_out, gwu_out, gwd_out))
    ]
    for copy in stores:
        copy.start()
    fin[octet] = sum_back(0)
    loop(experts - 1, lambda i: home(i).wait_recv())

    gathered = fin[...].reshape(deep, half + LANE)
    step = half // 2
    for h in range(2):
        for c in range(2):
            gt_ref[:, h * half + c * step : h * half + (c + 1) * step] = lax.dot_general(
                sel_ref[h], gathered[:, c * step : (c + 1) * step], FIRST, preferred_element_type=F32
            ).astype(BF16)
    dots = lax.dot_general(gathered[:, half:], sel_ref[0], FIRST, preferred_element_type=F32)
    gg_ref[...] = jnp.where(ids_ref[...] < experts, dots[: ids_ref.shape[0]], 0.0)

    def finish(d):
        for k in range(4):
            for p in range(2):
                ac(d, k, p).wait_send()
            back_core(d, k).wait_send()
        for k in (1, 2, 3):
            for p in range(2):
                a1(d, k, p).wait_send()
            back(d, k).wait_send()

    loop(experts, finish)

    def finish_far(i):
        for p in range(2):
            s1(i, p).wait_send()
        home(i).wait_send()

    loop(experts - 1, finish_far)
    for copy in stores:
        copy.wait()


def hand_over_kernel(cuts, *refs):
    count = len(cuts)
    sources, results, held = refs[:count], refs[count : 2 * count], refs[2 * count : 3 * count]
    in_sem, out_sem = refs[3 * count :]
    arrive, leave = [], []
    for i in range(count):
        size = sources[i].shape[0] // cuts[i]
        for c in range(cuts[i]):
            rows = pl.ds(c * size, size)
            n = len(arrive)
            arrive.append(pltpu.make_async_copy(sources[i].at[rows], held[i].at[rows], in_sem.at[n]))
            leave.append(pltpu.make_async_copy(held[i].at[rows], results[i].at[rows], out_sem.at[n]))
    for copy in arrive:
        copy.start()
    for copy, after in zip(arrive, leave):
        copy.wait()
        after.start()
    for copy in leave:
        copy.wait()


def local(tokens, grad_out, expert_ids, gate_weights, w_gate, w_up, w_down):
    flat_count = lax.axis_size(("expert", "dp"))
    experts = flat_count // SPAN
    count, features = tokens.shape
    hid = w_gate.shape[0]
    half = features // 2
    tiles = 4
    tile = features // tiles
    wide = 3 * tile + LANE
    deep = experts * ROWS
    ids_t, gates_t = expert_ids.T, gate_weights.T
    narrow = half + LANE
    slots = experts * SPAN
    far = max(experts - 1, 1)
    vmem = pl.BlockSpec(memory_space=pltpu.VMEM)
    anyspace = pl.BlockSpec(memory_space=pl.ANY)
    sem = pltpu.SemaphoreType.DMA
    full = jax.ShapeDtypeStruct((hid, features), BF16)
    made = pl.pallas_call(
        functools.partial(exchange_kernel, experts),
        out_shape=(
            jax.ShapeDtypeStruct((count, features), BF16),
            jax.ShapeDtypeStruct(gates_t.shape, F32),
            full, full, full,
        ),
        in_specs=[anyspace, anyspace, vmem, vmem, anyspace, anyspace, anyspace],
        out_specs=(vmem, vmem, anyspace, anyspace, anyspace),
        scratch_shapes=[
            pltpu.VMEM((2, deep, count), BF16),
            pltpu.VMEM((experts, ROWS, narrow), BF16),
            pltpu.VMEM((3 * hid, features), BF16),
            pltpu.VMEM((count, features), BF16),
            pltpu.VMEM((count, features), BF16),
            pltpu.VMEM((3 * hid, features), BF16),
            pltpu.VMEM((experts, ROWS, wide), BF16),
            pltpu.VMEM((slots, ROWS, wide), BF16),
            pltpu.VMEM((slots, ROWS, tile), BF16),
            pltpu.VMEM((slots, ROWS, 3 * hid), BF16),
            pltpu.VMEM((slots, ROWS, narrow), BF16),
            pltpu.VMEM((experts, 4, ROWS, narrow), BF16),
            pltpu.VMEM((experts, 3, ROWS, narrow), BF16),
            sem((7,)), sem((3,)),
            sem((far, 2)), sem((far, 2)),
            sem((experts, 3, 2)), sem((experts, 3, 2)),
            sem((experts, 4, 2)), sem((experts, 4, 2)),
            sem((experts, 4)), sem((experts, 4)),
            sem((experts, 3)), sem((experts, 3)),
            sem((far,)), sem((far,)),
        ],
        compiler_params=pltpu.CompilerParams(
            collective_id=0, has_side_effects=True, vmem_limit_bytes=60 * 1024 * 1024
        ),
    )(tokens, grad_out, ids_t, gates_t, w_gate, w_up, w_down)
    cuts = (2, 1, 2, 2, 2)
    grad_tokens, grad_gates, grad_gate, grad_up, grad_down = pl.pallas_call(
        functools.partial(hand_over_kernel, cuts),
        out_shape=tuple(jax.ShapeDtypeStruct(a.shape, a.dtype) for a in made),
        in_specs=[anyspace] * len(cuts),
        out_specs=(anyspace,) * len(cuts),
        scratch_shapes=[pltpu.VMEM(a.shape, a.dtype) for a in made] + [sem((sum(cuts),)), sem((sum(cuts),))],
        compiler_params=pltpu.CompilerParams(vmem_limit_bytes=60 * 1024 * 1024),
    )(*made)
    return grad_tokens, grad_gates.T, grad_gate, grad_up, grad_down


def solution(mesh):
    rows = P(("groups", "expert", "dp"), None)
    weights = P(("expert", "dp"), None)
    return jax.shard_map(
        local,
        mesh=mesh,
        in_specs=(rows,) * 4 + (weights,) * 3,
        out_specs=(rows,) * 5,
        check_vma=False,
    )
```
